32 devices in a mesh: seq: 8 (over z, core), chan: 4 (over y, x).
Axes of the slice: x: 2, y: 2, z: 4, core: 2. Of those that a mesh axis runs over, the one named last changes fastest.
Arguments:
- values: bfloat16 [2048, 4096], P('seq', 'chan'), may hold values from -6 to 6
- gates: bfloat16 [2048, 4096], P('seq', 'chan'), may hold values from -6 to 6
- filters: bfloat16 [1024, 4096], P(None, 'chan'), may hold values from -2 to 2
- skip: float32 [4096], P('chan'), may hold values from -4 to 4
- out_weight: bfloat16 [4096, 4096], P(('seq', 'chan')), may hold values from -0.09375 to 0.09375
Outputs:
- projected: bfloat16 [2048, 4096], P(('seq', 'chan'))
The draws below stay inside these ranges and needn't reach their ends.
All inputs are finite; a program needn't handle non-finite values.
Results may differ from the reference program's by a relative error of at most 0.009.
Values may be sent and summed in bfloat16 or wider, within the bound.
No kernel may reach another device: no remote copies, remote signals or barrier semaphores. Data moves between devices by JAX's collectives and lax.ppermute only.
A program may use at most 192 MiB of HBM per device.

```python
import math
import jax
import jax.numpy as jnp
from jax import lax

D = 4096
FILT = 1024
TOKENS = 2048


def draw_filters(key, part):
    key_noise, key_rate = jax.random.split(jax.random.fold_in(key, 17))
    lagged = jnp.arange(FILT, dtype=jnp.float32)[:, None]
    noise = jnp.clip(jax.random.normal(key_noise, (FILT, D), jnp.float32), -6.0, 6.0)
    log_rate = jax.random.uniform(key_rate, (1, D), jnp.float32, math.log(0.05 / FILT), math.log(1.0 / 30.0))
    rate = jnp.exp(log_rate)
    scale = jnp.sqrt(jnp.expm1(-2.0 * rate) / jnp.expm1(-2.0 * rate * FILT))
    return (noise * jnp.exp(-rate * lagged) * scale).astype(jnp.bfloat16)


def block_levels(key, dims, cuts, low, top_value):
    level = 1.0
    for axis_at, blocks in cuts:
        steps = jax.random.uniform(jax.random.fold_in(jax.random.fold_in(key, 6), axis_at), (blocks,), jnp.float32, low / len(cuts), top_value / len(cuts))
        level = level * jnp.repeat(jnp.exp(steps), dims[axis_at] // blocks).reshape((-1,) + (1,) * (len(dims) - 1 - axis_at))
    return level


def centred(stream_key, extent, deviation, limit, pieces=(), held_as=jnp.bfloat16):
    gain = block_levels(stream_key, extent, pieces, -0.22, 0.18) if pieces else 1.0
    result = jax.random.normal(stream_key, extent, jnp.float32) * deviation * gain
    return jnp.minimum(jnp.maximum(result, -limit), limit).astype(held_as)


def setup_inputs(seed: int = 0) -> dict:
    keys = jax.random.split(jax.random.key(seed), 6)
    values = centred(keys[0], (TOKENS, D), 1.0, 6.0, ((0, 8), (1, 4)))
    gates = centred(keys[1], (TOKENS, D), 1.0, 6.0, ((0, 8), (1, 4)))
    filters = draw_filters(jax.random.fold_in(keys[5], 71), 0)
    skip = centred(keys[3], (D,), 1.0, 4.0, ((0, 4),), jnp.float32)
    out_weight = centred(keys[4], (D, D), D ** -0.5, 0.09375, ((0, 32),))
    return {"values": values, "gates": gates, "filters": filters, "skip": skip, "out_weight": out_weight}


def reference(values, gates, filters, skip, out_weight):
    length = values.shape[0]
    width = values.shape[1]
    group = math.gcd(width, 512)
    count = width // group
    period = 2 * length

    def split_groups(array):
        return jnp.transpose(array.reshape(array.shape[0], count, group), (1, 0, 2))

    def one_group(operands):
        value_part, gate_part, filter_part, skip_part = operands
        value_float = value_part.astype(jnp.float32)
        spectrum = jnp.fft.rfft(value_float, n=period, axis=0) * jnp.fft.rfft(filter_part.astype(jnp.float32), n=period, axis=0)
        convolved = jnp.fft.irfft(spectrum, n=period, axis=0)[:length]
        filtered = convolved + skip_part[None, :] * value_float
        return (gate_part.astype(jnp.float32) * filtered).astype(jnp.bfloat16)

    gated = lax.map(one_group, (split_groups(values), split_groups(gates), split_groups(filters), skip.reshape(count, group)))
    gated = jnp.transpose(gated, (1, 0, 2)).reshape(length, width)
    return jnp.dot(gated, out_weight, preferred_element_type=jnp.float32).astype(jnp.bfloat16)
```

```python
import functools
import math

import jax
import jax.numpy as jnp
from jax import lax
from jax.experimental import pallas as pl
from jax.experimental.pallas import tpu as pltpu
from jax.sharding import PartitionSpec as P

AXES = ("seq", "chan")
F32 = jnp.float32
BF16 = jnp.bfloat16


def permute(value, move):
    pairs, chans = lax.axis_size("seq") // 2, lax.axis_size("chan")
    route = []
    for pair in range(pairs):
        for core in range(2):
            for chan in range(chans):
                target = move(pair, core, chan)
                if target is not None and 0 <= target[0] < pairs:
                    route.append(
                        (
                            (pair * 2 + core) * chans + chan,
                            (target[0] * 2 + target[1]) * chans + target[2],
                        )
                    )
    return lax.ppermute(value, AXES, route)


def tables(block):
    order = jnp.concatenate([jnp.arange(0, block, 2), jnp.arange(1, block, 2)])
    phase = (2 * order[:, None] + 1) * jnp.arange(block)[None, :] % (4 * block)
    angle = phase.astype(F32) * (math.pi / (2 * block))
    return jnp.concatenate([jnp.cos(angle), jnp.sin(angle)], axis=0)


def conv_kernel(lags, core_ref, table_ref, back_ref, skip_ref, gates_ref, filters_ref, *rest):
    *block_refs, out_ref = rest
    block = gates_ref.shape[0]
    half = block // 2
    odd = core_ref[0] == 1
    reach = lags // 2

    def transform(operand):
        return jnp.dot(table_ref[...], operand, preferred_element_type=F32)

    direct = block_refs[: reach + 1]
    crossed = block_refs[reach + 1 :]
    cos_parts, sin_parts = [], []
    for lag in range(lags + 1):
        if lag % 2 == 0:
            operand = direct[lag // 2][...]
        else:
            operand = jnp.where(odd, crossed[lag // 2][...], crossed[lag // 2 + 1][...])
        both = transform(operand)
        cos_parts.append(both[:block])
        sin_parts.append(both[block:])
    real = imag = 0.0
    for lag in range(lags):
        both = transform(filters_ref[lag * block : (lag + 1) * block, :])
        tap_cos, tap_sin = both[:block], both[block:]
        near_cos, near_sin = cos_parts[lag], sin_parts[lag]
        far_cos, far_sin = cos_parts[lag + 1], sin_parts[lag + 1]
        window_cos = jnp.concatenate(
            [near_cos[:half] + far_sin[:half], near_cos[half:] - far_sin[half:]], axis=0
        )
        window_sin = jnp.concatenate(
            [near_sin[:half] - far_cos[:half], near_sin[half:] + far_cos[half:]], axis=0
        )
        real = real + tap_cos * window_cos - tap_sin * window_sin
        imag = imag + tap_cos * window_sin + tap_sin * window_cos
    spectrum = jnp.concatenate([real, imag], axis=0).astype(BF16)
    filtered = jnp.dot(back_ref[...], spectrum, preferred_element_type=F32) * (1.0 / block)
    filtered = filtered + skip_ref[...] * direct[0][...].astype(F32)
    out_ref[...] = (gates_ref[...].astype(F32) * filtered).astype(BF16)


def convolve(core, gates, filters, skip, direct, crossed):
    block, width = gates.shape
    taps = filters.shape[0]
    lags = taps // block
    table = tables(block)
    tile = min(width, 256)

    def column(rows):
        return pl.BlockSpec((rows, tile), lambda i, *_: (0, i))

    def whole(rows, cols):
        return pl.BlockSpec((rows, cols), lambda i, *_: (0, 0))

    blocks = [*direct, *crossed]
    return pl.pallas_call(
        functools.partial(conv_kernel, lags),
        grid_spec=pltpu.PrefetchScalarGridSpec(
            num_scalar_prefetch=1,
            grid=(width // tile,),
            in_specs=[
                whole(2 * block, block),
                whole(block, 2 * block),
                column(1),
                column(block),
                column(taps),
                *[column(block) for _ in blocks],
            ],
            out_specs=column(block),
        ),
        out_shape=jax.ShapeDtypeStruct((block, width), BF16),
        compiler_params=pltpu.CompilerParams(vmem_limit_bytes=40 * 2**20),
        cost_estimate=pl.CostEstimate(
            flops=2 * (3 * lags + 3) * 2 * block * block * width,
            bytes_accessed=2 * width * (taps + (len(blocks) + 2) * block),
            transcendentals=0,
        ),
        name="conv",
    )(
        core.reshape(1),
        table.astype(BF16),
        table.T.astype(BF16),
        skip.reshape(1, width),
        gates,
        filters,
        *blocks,
    )


def project_kernel(count, offsets_ref, *refs):
    act_refs, piece_refs = refs[:count], refs[count : 2 * count]
    out_ref, held_ref = refs[2 * count :]
    rows = act_refs[0].shape[0]
    depth = piece_refs[0].shape[0] // 2

    @pl.when(pl.program_id(0) == 0)
    def _():
        for index, act in enumerate(act_refs):
            if depth % 128:
                held_ref[index * rows : (index + 1) * rows, :] = act[...]
                continue
            for slot in range(2 * count):
                start = pl.multiple_of(offsets_ref[slot], depth)
                held_ref[index * rows : (index + 1) * rows, slot * depth : (slot + 1) * depth] = (
                    act[:, pl.ds(start, depth)]
                )

    weight = jnp.concatenate([piece[...] for piece in piece_refs], axis=0)
    out_ref[...] = jnp.dot(held_ref[...], weight, preferred_element_type=F32)


def project(offsets, acts, pieces):
    count = len(acts)
    rows, depth = acts[0].shape
    cols = pieces[0].shape[1]
    tile = min(cols, 512)
    slot = depth // (2 * count)
    if slot % 128:
        acts = [
            jnp.concatenate(
                [
                    lax.dynamic_slice_in_dim(act, offsets[index], slot, axis=1)
                    for index in range(2 * count)
                ],
                axis=1,
            )
            for act in acts
        ]
    return pl.pallas_call(
        functools.partial(project_kernel, count),
        grid_spec=pltpu.PrefetchScalarGridSpec(
            num_scalar_prefetch=1,
            grid=(cols // tile,),
            in_specs=[
                *[pl.BlockSpec((rows, depth), lambda i, *_: (0, 0)) for _ in acts],
                *[
                    pl.BlockSpec((piece.shape[0], tile), lambda i, *_: (0, i))
                    for piece in pieces
                ],
            ],
            out_specs=pl.BlockSpec((count * rows, tile), lambda i, *_: (0, i)),
            scratch_shapes=[pltpu.VMEM((count * rows, depth), BF16)],
        ),
        out_shape=jax.ShapeDtypeStruct((count * rows, cols), F32),
        compiler_params=pltpu.CompilerParams(vmem_limit_bytes=40 * 2**20),
        cost_estimate=pl.CostEstimate(
            flops=2 * count * rows * depth * cols,
            bytes_accessed=2 * depth * cols + 6 * count * rows * cols,
            transcendentals=0,
        ),
        name="project",
    )(offsets, *acts, *pieces)


def body(values, gates, filters, skip, out_weight):
    pairs, chans = lax.axis_size("seq") // 2, lax.axis_size("chan")
    seq, chan = lax.axis_index("seq"), lax.axis_index("chan")
    pair, core = seq // 2, seq % 2
    block = values.shape[0]
    lags = filters.shape[0] // block
    own_rows, model = out_weight.shape
    half = model // 2

    mine = lax.dynamic_slice_in_dim(out_weight, core * half, half, axis=1)
    other = lax.dynamic_slice_in_dim(out_weight, (1 - core) * half, half, axis=1)

    direct = [values]
    for _ in range(lags // 2):
        direct.append(permute(direct[-1], lambda p, k, c: (p + 1, k, c)))
    crossed = [permute(held, lambda p, k, c: (p, 1 - k, c)) for held in direct]

    swapped = permute(other, lambda p, k, c: (p, 1 - k, c))
    pieces = [jnp.concatenate([mine, swapped], axis=0)]
    for step in range(1, chans):
        pieces.append(permute(pieces[0], lambda p, k, c, step=step: (p, k, c ^ step)))
    far_pieces = [permute(piece, lambda p, k, c: (p, 1 - k, c)) for piece in pieces]

    gated = convolve(core, gates, filters, skip, direct, crossed)

    rows = block // chans
    acts = []
    for step in range(chans):
        part = lax.dynamic_slice_in_dim(gated, (pair + step) % chans * rows, rows, axis=0)
        acts.append(permute(part, lambda p, k, c, step=step: (c, k, (p + step) % chans)))

    def offsets(first):
        return jnp.stack(
            [
                (which * chans + (chan ^ step)) * own_rows
                for step in range(chans)
                for which in (first, 1 - first)
            ]
        ).astype(jnp.int32)

    totals = []
    for first, weight in ((core, pieces), (1 - core, far_pieces)):
        partial = project(offsets(first), acts, weight).reshape(chans, rows, half)

        def share(target, partial=partial):
            return lax.dynamic_index_in_dim(
                partial, (chan - target) % chans, axis=0, keepdims=False
            )

        up = down = None
        for step in range(1, pairs):
            send_up = share(pairs + pair - step)
            send_down = share(pair - pairs + step)
            if step > 1:
                send_up = send_up + up.astype(F32)
                send_down = send_down + down.astype(F32)
            up = permute(
                send_up.astype(BF16),
                lambda p, k, c, step=step: (p + 1, k, c) if p < step else None,
            )
            down = permute(
                send_down.astype(BF16),
                lambda p, k, c, step=step: (p - 1, k, c) if pairs - 1 - p < step else None,
            )
        totals.append((share(pair) + up.astype(F32) + down.astype(F32)).astype(BF16))
    swap = core == 1
    return jnp.concatenate(
        [jnp.where(swap, totals[1], totals[0]), jnp.where(swap, totals[0], totals[1])], axis=1
    )


def solution(mesh):
    in_specs = (
        P("seq", "chan"),
        P("seq", "chan"),
        P(None, "chan"),
        P("chan"),
        P(("seq", "chan"), None),
    )
    out_specs = P(("seq", "chan"), None)
    return jax.shard_map(body, mesh=mesh, in_specs=in_specs, out_specs=out_specs, check_vma=False)
```

```python
import functools
import math

import jax
import jax.numpy as jnp
import numpy as np
from jax import lax
from jax.experimental import pallas as pl
from jax.experimental.pallas import tpu as pltpu
from jax.sharding import PartitionSpec as P

AXES = ("seq", "chan")
F32 = jnp.float32
BF16 = jnp.bfloat16


def sizes():
    return lax.axis_size("seq") // 2, lax.axis_size("chan")


def place(pairs, chans, pair, core, chan):
    return (pair * 2 + core) * chans + chan


def permute(value, move):
    pairs, chans = sizes()
    route = []
    for pair in range(pairs):
        for core in range(2):
            for chan in range(chans):
                target = move(pair, core, chan)
                if target is not None and 0 <= target[0] < pairs:
                    route.append(
                        (place(pairs, chans, pair, core, chan), place(pairs, chans, *target))
                    )
    return lax.ppermute(value, AXES, route)


def table(block):
    order = np.concatenate([np.arange(0, block, 2), np.arange(1, block, 2)])
    phase = (2 * order[:, None] + 1) * np.arange(block)[None, :] % (4 * block)
    angle = phase * (math.pi / (2 * block))
    return np.concatenate([np.cos(angle), np.sin(angle)], axis=0)


def conv_kernel(lags, core_ref, table_ref, back_ref, skip_ref, gates_ref, filters_ref, *rest):
    *block_refs, out_ref = rest
    block = gates_ref.shape[0]
    half = block // 2
    odd = core_ref[0] == 1
    reach = lags // 2

    def transform(operand):
        return jnp.dot(table_ref[...], operand, preferred_element_type=F32)

    direct = block_refs[: reach + 1]
    crossed = block_refs[reach + 1 :]
    cos_parts, sin_parts = [], []
    for lag in range(lags + 1):
        if lag % 2 == 0:
            operand = direct[lag // 2][...]
        else:
            operand = jnp.where(odd, crossed[lag // 2][...], crossed[lag // 2 + 1][...])
        both = transform(operand)
        cos_parts.append(both[:block])
        sin_parts.append(both[block:])
    real = imag = 0.0
    for lag in range(lags):
        both = transform(filters_ref[lag * block : (lag + 1) * block, :])
        tap_cos, tap_sin = both[:block], both[block:]
        near_cos, near_sin = cos_parts[lag], sin_parts[lag]
        far_cos, far_sin = cos_parts[lag + 1], sin_parts[lag + 1]
        window_cos = jnp.concatenate(
            [near_cos[:half] + far_sin[:half], near_cos[half:] - far_sin[half:]], axis=0
        )
        window_sin = jnp.concatenate(
            [near_sin[:half] - far_cos[:half], near_sin[half:] + far_cos[half:]], axis=0
        )
        real = real + tap_cos * window_cos - tap_sin * window_sin
        imag = imag + tap_cos * window_sin + tap_sin * window_cos
    spectrum = jnp.concatenate([real, imag], axis=0).astype(BF16)
    filtered = jnp.dot(back_ref[...], spectrum, preferred_element_type=F32) * (1.0 / block)
    filtered = filtered + skip_ref[...] * direct[0][...].astype(F32)
    out_ref[...] = (gates_ref[...].astype(F32) * filtered).astype(BF16)


def convolve(core, gates, filters, skip, direct, crossed):
    block, width = gates.shape
    taps = filters.shape[0]
    lags = taps // block
    forth = table(block)
    tile = min(width, 256)

    def column(rows):
        return pl.BlockSpec((rows, tile), lambda i, *_: (0, i))

    def whole(rows, cols):
        return pl.BlockSpec((rows, cols), lambda i, *_: (0, 0))

    blocks = [*direct, *crossed]
    return pl.pallas_call(
        functools.partial(conv_kernel, lags),
        grid_spec=pltpu.PrefetchScalarGridSpec(
            num_scalar_prefetch=1,
            grid=(width // tile,),
            in_specs=[
                whole(2 * block, block),
                whole(block, 2 * block),
                column(1),
                column(block),
                column(taps),
                *[column(block) for _ in blocks],
            ],
            out_specs=column(block),
        ),
        out_shape=jax.ShapeDtypeStruct((block, width), BF16),
        cost_estimate=pl.CostEstimate(
            flops=2 * (3 * lags + 3) * 2 * block * block * width,
            bytes_accessed=2 * width * (taps + (len(blocks) + 2) * block),
            transcendentals=0,
        ),
        name="conv",
    )(
        core.reshape(1),
        jnp.asarray(forth, BF16),
        jnp.asarray(forth.T, BF16),
        skip.reshape(1, width),
        gates,
        filters,
        *blocks,
    )


def join_kernel(count, *refs):
    out_ref = refs[-1]
    start = 0
    for ref in refs[:count]:
        out_ref[start : start + ref.shape[0], :] = ref[...]
        start += ref.shape[0]


def join(parts, cols, deps=()):
    rows = sum(array.shape[0] for array, _ in parts)
    return pl.pallas_call(
        functools.partial(join_kernel, len(parts)),
        grid=(1,),
        in_specs=[
            *[
                pl.BlockSpec((array.shape[0], cols), lambda i, index=index: (0, index))
                for array, index in parts
            ],
            *[pl.BlockSpec(memory_space=pl.ANY) for _ in deps],
        ],
        out_specs=pl.BlockSpec((rows, cols), lambda i: (0, 0)),
        out_shape=jax.ShapeDtypeStruct((rows, cols), BF16),
        compiler_params=pltpu.CompilerParams(vmem_limit_bytes=12 * 2**20),
        name="join",
    )(*[array for array, _ in parts], *deps)


def part_kernel(many, index_ref, from_ref, *refs):
    for step, ref in enumerate(refs[-many:]):
        ref[...] = from_ref[index_ref[0] ^ step]


def part(index, array, deps):
    many, rows, depth = array.shape
    return pl.pallas_call(
        functools.partial(part_kernel, many),
        grid_spec=pltpu.PrefetchScalarGridSpec(
            num_scalar_prefetch=1,
            grid=(1,),
            in_specs=[pl.BlockSpec(array.shape, lambda i, *_: (0, 0, 0))]
            + [pl.BlockSpec(memory_space=pl.ANY)] * len(deps),
            out_specs=[pl.BlockSpec((rows, depth), lambda i, *_: (0, 0))] * many,
        ),
        out_shape=[jax.ShapeDtypeStruct((rows, depth), BF16)] * many,
        compiler_params=pltpu.CompilerParams(vmem_limit_bytes=12 * 2**20),
        name="part",
    )(index.reshape(1), array, *deps)


def fence_kernel(*refs):
    del refs


def fence(arrays, deps):
    anywhere = pl.BlockSpec(memory_space=pl.ANY)
    return pl.pallas_call(
        fence_kernel,
        in_specs=[anywhere] * (len(arrays) + len(deps)),
        out_specs=[anywhere] * len(arrays),
        out_shape=[jax.ShapeDtypeStruct(array.shape, array.dtype) for array in arrays],
        input_output_aliases={index: index for index in range(len(arrays))},
        name="fence",
    )(*arrays, *deps)


def arrange_kernel(slots, order_ref, *refs):
    out_ref = refs[-1]
    rows, depth = refs[0].shape
    width = depth // slots
    for index, ref in enumerate(refs[:-1]):
        here = slice(index * rows, (index + 1) * rows)
        if width % 128:
            out_ref[here, :] = ref[...]
            continue
        for slot in range(slots):
            start = pl.multiple_of(order_ref[slot] * width, width)
            out_ref[here, slot * width : (slot + 1) * width] = ref[:, pl.ds(start, width)]


def arrange(order, acts):
    slots = order.shape[0]
    rows, depth = acts[0].shape
    width = depth // slots
    if width % 128:
        acts = [
            jnp.concatenate(
                [
                    lax.dynamic_slice_in_dim(act, order[slot] * width, width, axis=1)
                    for slot in range(slots)
                ],
                axis=1,
            )
            for act in acts
        ]
    return pl.pallas_call(
        functools.partial(arrange_kernel, slots),
        grid_spec=pltpu.PrefetchScalarGridSpec(
            num_scalar_prefetch=1,
            grid=(1,),
            in_specs=[pl.BlockSpec((rows, depth), lambda i, *_: (0, 0)) for _ in acts],
            out_specs=pl.BlockSpec((rows * len(acts), depth), lambda i, *_: (0, 0)),
        ),
        out_shape=jax.ShapeDtypeStruct((rows * len(acts), depth), BF16),
        compiler_params=pltpu.CompilerParams(vmem_limit_bytes=12 * 2**20),
        name="arrange",
    )(order, *acts)


def project_kernel(spots, width, acts_ref, *refs):
    piece_refs = refs[:-2]
    send_ref, keep_ref = refs[-2:]
    rows = acts_ref.shape[0] // 2
    weight = jnp.concatenate(
        [piece_refs[piece][spot * width : (spot + 1) * width, :] for piece, spot in spots], axis=0
    )
    total = jnp.dot(acts_ref[...], weight, preferred_element_type=F32)
    send_ref[...] = total[:rows].astype(BF16)
    keep_ref[...] = total[rows:]


def project(acts, pieces, spots, width, cols):
    count, depth = acts.shape
    tile = min(cols, 512)
    return pl.pallas_call(
        functools.partial(project_kernel, spots, width),
        grid=(cols // tile,),
        in_specs=[
            pl.BlockSpec((count, depth), lambda i: (0, 0)),
            *[
                pl.BlockSpec(
                    (piece.shape[0], tile), lambda i, first=first * cols // tile: (0, first + i)
                )
                for piece, first in pieces
            ],
        ],
        out_specs=[pl.BlockSpec((count // 2, tile), lambda i: (0, i))] * 2,
        out_shape=[
            jax.ShapeDtypeStruct((count // 2, cols), BF16),
            jax.ShapeDtypeStruct((count // 2, cols), F32),
        ],
        compiler_params=pltpu.CompilerParams(vmem_limit_bytes=16 * 2**20),
        cost_estimate=pl.CostEstimate(
            flops=2 * count * depth * cols,
            bytes_accessed=2 * depth * cols + 6 * count * cols,
            transcendentals=0,
        ),
        name="project",
    )(acts, *[piece for piece, _ in pieces])


def body(values, gates, filters, skip, out_weight):
    pairs, chans = sizes()
    seq, chan = lax.axis_index("seq"), lax.axis_index("chan")
    pair, core = seq // 2, seq % 2
    block = values.shape[0]
    lags = filters.shape[0] // block
    own_rows, model = out_weight.shape
    half = model // 2
    rows = block // chans

    def swap(array):
        return permute(array, lambda p, k, c: (p, 1 - k, c))

    direct = [values]
    for _ in range(lags // 2):
        direct.append(permute(direct[-1], lambda p, k, c: (p + 1, k, c)))
    crossed = [
        permute(
            held,
            lambda p, k, c, first=index == 0, last=index == lags // 2: None
            if (first and k == 1) or (last and k == 0)
            else (p, 1 - k, c),
        )
        for index, held in enumerate(direct)
    ]

    bits = [1 << index for index in range(chans.bit_length() - 1)]
    parts, spots = [], []
    for which, order in enumerate((bits, bits[::-1])):
        held = join([(out_weight, which)], half, [crossed[0]])
        found = [0]
        for step, bit in enumerate(order):
            if step:
                held = join([(piece, 0) for piece in pieces], half)
            pieces = [held, permute(held, lambda p, k, c, bit=bit: (p, k, c ^ bit))]
            found = found + [mask ^ bit for mask in found]
        parts.append(pieces)
        each = len(found) // 2
        spots.append(
            [
                (2 * other + found.index(mask) // each, found.index(mask) % each)
                for other in range(2)
                for mask in range(chans)
            ]
        )

    gated = convolve(core, gates, filters, skip, direct, crossed)

    spread = lax.all_to_all(
        gated.reshape(chans, rows, gated.shape[1]), "chan", split_axis=0, concat_axis=0
    )
    flat = fence([piece for pieces in parts for piece in pieces], [gated])
    parts = [flat[:2], flat[2:]]
    swaps = [[swap(piece) for piece in pieces] for pieces in parts]
    parts = [[*pieces, *others] for pieces, others in zip(parts, swaps, strict=True)]
    acts = list(part(pair, spread, [other for others in swaps for other in others]))
    for step in range(1, pairs):
        acts[step] = permute(acts[step], lambda p, k, c, step=step: (p ^ step, k, c))

    count = pairs.bit_length() - 1
    steps = [1 << index for index in range(count)]
    ranks = sorted(range(pairs), key=lambda e: [not e & step for step in steps])
    order = jnp.stack(
        [which * chans + (chan ^ mask) for which in (core, 1 - core) for mask in range(chans)]
    ).astype(jnp.int32)
    acts = arrange(order, [acts[rank] for rank in ranks])

    chunks = 4
    cols = model // chunks
    outs = []
    for chunk in range(chunks):
        which = chunk // 2
        send, keep = project(
            acts, [(piece, chunk % 2) for piece in parts[which]], spots[which], own_rows, cols
        )
        for index, step in enumerate(steps):
            got = permute(send, lambda p, k, c, step=step: (p ^ step, k, c)).astype(F32)
            many = got.shape[0] // 2
            if index + 1 < count:
                send = (keep[:many] + got[:many]).astype(BF16)
                keep = keep[many:] + got[many:]
            else:
                keep = keep + got
        outs.append(keep.astype(BF16))
    return jnp.concatenate(outs, axis=1)


def solution(mesh):
    in_specs = (
        P("seq", "chan"),
        P("seq", "chan"),
        P(None, "chan"),
        P("chan"),
        P(("seq", "chan"), None),
    )
    out_specs = P(("seq", "chan"), None)
    return jax.shard_map(body, mesh=mesh, in_specs=in_specs, out_specs=out_specs, check_vma=False)
```

```python
import functools
import math

import jax
import jax.numpy as jnp
import numpy as np
from jax import lax
from jax.experimental import pallas as pl
from jax.experimental.pallas import tpu as pltpu
from jax.sharding import PartitionSpec as P

AXES = ("seq", "chan")
F32 = jnp.float32
BF16 = jnp.bfloat16


def sizes():
    return lax.axis_size("seq") // 2, lax.axis_size("chan")


def place(pairs, chans, pair, core, chan):
    return (pair * 2 + core) * chans + chan


def permute(value, move):
    pairs, chans = sizes()
    route = []
    for pair in range(pairs):
        for core in range(2):
            for chan in range(chans):
                target = move(pair, core, chan)
                if target is not None and 0 <= target[0] < pairs:
                    route.append(
                        (place(pairs, chans, pair, core, chan), place(pairs, chans, *target))
                    )
    return lax.ppermute(value, AXES, route)


def table(block):
    order = np.concatenate([np.arange(0, block, 2), np.arange(1, block, 2)])
    phase = (2 * order[:, None] + 1) * np.arange(block)[None, :] % (4 * block)
    angle = phase * (math.pi / (2 * block))
    return np.concatenate([np.cos(angle), np.sin(angle)], axis=0)


def conv_kernel(lags, core_ref, table_ref, back_ref, skip_ref, gates_ref, filters_ref, *rest):
    block_refs, out_ref = rest[: lags + 2], rest[-1]
    block = gates_ref.shape[0]
    half = block // 2
    odd = core_ref[0] == 1
    reach = lags // 2

    def transform(operand):
        return jnp.dot(table_ref[...], operand, preferred_element_type=F32)

    direct = block_refs[: reach + 1]
    crossed = block_refs[reach + 1 :]
    cos_parts, sin_parts = [], []
    for lag in range(lags + 1):
        if lag % 2 == 0:
            operand = direct[lag // 2][...]
        else:
            operand = jnp.where(odd, crossed[lag // 2][...], crossed[lag // 2 + 1][...])
        both = transform(operand)
        cos_parts.append(both[:block])
        sin_parts.append(both[block:])
    real = imag = 0.0
    for lag in range(lags):
        both = transform(filters_ref[lag * block : (lag + 1) * block, :])
        tap_cos, tap_sin = both[:block], both[block:]
        near_cos, near_sin = cos_parts[lag], sin_parts[lag]
        far_cos, far_sin = cos_parts[lag + 1], sin_parts[lag + 1]
        window_cos = jnp.concatenate(
            [near_cos[:half] + far_sin[:half], near_cos[half:] - far_sin[half:]], axis=0
        )
        window_sin = jnp.concatenate(
            [near_sin[:half] - far_cos[:half], near_sin[half:] + far_cos[half:]], axis=0
        )
        real = real + tap_cos * window_cos - tap_sin * window_sin
        imag = imag + tap_cos * window_sin + tap_sin * window_cos
    spectrum = jnp.concatenate([real, imag], axis=0).astype(BF16)
    filtered = jnp.dot(back_ref[...], spectrum, preferred_element_type=F32) * (1.0 / block)
    filtered = filtered + skip_ref[...] * direct[0][...].astype(F32)
    out_ref[...] = (gates_ref[...].astype(F32) * filtered).astype(BF16)


def convolve(core, gates, filters, skip, direct, crossed, deps):
    block, width = gates.shape
    taps = filters.shape[0]
    lags = taps // block
    forth = table(block)
    tile = min(width, 256)

    def column(rows):
        return pl.BlockSpec((rows, tile), lambda i, *_: (0, i))

    def whole(rows, cols):
        return pl.BlockSpec((rows, cols), lambda i, *_: (0, 0))

    blocks = [*direct, *crossed]
    return pl.pallas_call(
        functools.partial(conv_kernel, lags),
        grid_spec=pltpu.PrefetchScalarGridSpec(
            num_scalar_prefetch=1,
            grid=(width // tile,),
            in_specs=[
                whole(2 * block, block),
                whole(block, 2 * block),
                column(1),
                column(block),
                column(taps),
                *[column(block) for _ in blocks],
                *[pl.BlockSpec(memory_space=pl.ANY) for _ in deps],
            ],
            out_specs=column(block),
        ),
        out_shape=jax.ShapeDtypeStruct((block, width), BF16),
        cost_estimate=pl.CostEstimate(
            flops=2 * (3 * lags + 3) * 2 * block * block * width,
            bytes_accessed=2 * width * (taps + (len(blocks) + 2) * block),
            transcendentals=0,
        ),
        name="conv",
    )(
        core.reshape(1),
        jnp.asarray(forth, BF16),
        jnp.asarray(forth.T, BF16),
        skip.reshape(1, width),
        gates,
        filters,
        *blocks,
        *deps,
    )


def join_kernel(count, *refs):
    out_ref = refs[-1]
    start = 0
    for ref in refs[:count]:
        out_ref[start : start + ref.shape[0], :] = ref[...]
        start += ref.shape[0]


def join(parts, cols, deps=()):
    rows = sum(array.shape[0] for array, _ in parts)
    return pl.pallas_call(
        functools.partial(join_kernel, len(parts)),
        grid=(1,),
        in_specs=[
            *[
                pl.BlockSpec((array.shape[0], cols), lambda i, index=index: (0, index))
                for array, index in parts
            ],
            *[pl.BlockSpec(memory_space=pl.ANY) for _ in deps],
        ],
        out_specs=pl.BlockSpec((rows, cols), lambda i: (0, 0)),
        out_shape=jax.ShapeDtypeStruct((rows, cols), BF16),
        compiler_params=pltpu.CompilerParams(vmem_limit_bytes=12 * 2**20),
        name="join",
    )(*[array for array, _ in parts], *deps)


def part_kernel(many, slots, order_ref, from_ref, *refs):
    width = from_ref.shape[2] // slots
    for step, ref in enumerate(refs):
        here = order_ref[slots] ^ step
        if width % 128:
            ref[...] = from_ref[here]
            continue
        for slot in range(slots):
            start = pl.multiple_of(order_ref[slot] * width, width)
            ref[:, slot * width : (slot + 1) * width] = from_ref[here, :, pl.ds(start, width)]


def part(order, array):
    many, rows, depth = array.shape
    slots = order.shape[0] - 1
    width = depth // slots
    if width % 128:
        array = jnp.concatenate(
            [
                lax.dynamic_slice_in_dim(array, order[slot] * width, width, axis=2)
                for slot in range(slots)
            ],
            axis=2,
        )
    return list(
        pl.pallas_call(
            functools.partial(part_kernel, many, slots),
            grid_spec=pltpu.PrefetchScalarGridSpec(
                num_scalar_prefetch=1,
                grid=(1,),
                in_specs=[pl.BlockSpec(array.shape, lambda i, *_: (0, 0, 0))],
                out_specs=[pl.BlockSpec((rows, depth), lambda i, *_: (0, 0))] * many,
            ),
            out_shape=[jax.ShapeDtypeStruct((rows, depth), BF16)] * many,
            compiler_params=pltpu.CompilerParams(vmem_limit_bytes=12 * 2**20),
            name="part",
        )(order, array)
    )


def fence_kernel(*refs):
    del refs


def fence(arrays, deps):
    anywhere = pl.BlockSpec(memory_space=pl.ANY)
    return pl.pallas_call(
        fence_kernel,
        in_specs=[anywhere] * (len(arrays) + len(deps)),
        out_specs=[anywhere] * len(arrays),
        out_shape=[jax.ShapeDtypeStruct(array.shape, array.dtype) for array in arrays],
        input_output_aliases={index: index for index in range(len(arrays))},
        name="fence",
    )(*arrays, *deps)


def project_kernel(count, spots, width, *refs):
    act_refs, piece_refs = refs[:count], refs[count:-2]
    send_ref, keep_ref = refs[-2:]
    rows = send_ref.shape[0]
    weight = jnp.concatenate(
        [piece_refs[piece][spot * width : (spot + 1) * width, :] for piece, spot in spots], axis=0
    )
    acts = jnp.concatenate([act[...] for act in act_refs], axis=0)
    total = jnp.dot(acts, weight, preferred_element_type=F32)
    send_ref[...] = total[:rows].astype(BF16)
    keep_ref[...] = total[rows:]


def project(acts, pieces, spots, width, cols):
    rows, depth = acts[0].shape
    count = rows * len(acts)
    tile = min(cols, 512)
    return pl.pallas_call(
        functools.partial(project_kernel, len(acts), spots, width),
        grid=(cols // tile,),
        in_specs=[
            *[pl.BlockSpec((rows, depth), lambda i: (0, 0)) for _ in acts],
            *[
                pl.BlockSpec(
                    (piece.shape[0], tile), lambda i, first=first * cols // tile: (0, first + i)
                )
                for piece, first in pieces
            ],
        ],
        out_specs=[pl.BlockSpec((count // 2, tile), lambda i: (0, i))] * 2,
        out_shape=[
            jax.ShapeDtypeStruct((count // 2, cols), BF16),
            jax.ShapeDtypeStruct((count // 2, cols), F32),
        ],
        compiler_params=pltpu.CompilerParams(vmem_limit_bytes=16 * 2**20),
        cost_estimate=pl.CostEstimate(
            flops=2 * count * depth * cols,
            bytes_accessed=2 * depth * cols + 6 * count * cols,
            transcendentals=0,
        ),
        name="project",
    )(*acts, *[piece for piece, _ in pieces])


def body(values, gates, filters, skip, out_weight):
    pairs, chans = sizes()
    seq, chan = lax.axis_index("seq"), lax.axis_index("chan")
    pair, core = seq // 2, seq % 2
    block = values.shape[0]
    lags = filters.shape[0] // block
    own_rows, model = out_weight.shape
    half = model // 2
    rows = block // chans

    def swap(array):
        return permute(array, lambda p, k, c: (p, 1 - k, c))

    direct = [values]
    for _ in range(lags // 2):
        direct.append(permute(direct[-1], lambda p, k, c: (p + 1, k, c)))
    crossed = [
        permute(
            held,
            lambda p, k, c, first=index == 0, last=index == lags // 2: None
            if (first and k == 1) or (last and k == 0)
            else (p, 1 - k, c),
        )
        for index, held in enumerate(direct)
    ]

    bits = [1 << index for index in range(chans.bit_length() - 1)]
    parts, spots = [], []
    for which, order in enumerate((bits, bits[::-1])):
        held = join([(out_weight, which)], half, [crossed[0]])
        found = [0]
        for step, bit in enumerate(order):
            if step:
                held = join([(piece, 0) for piece in pieces], half)
            pieces = [held, permute(held, lambda p, k, c, bit=bit: (p, k, c ^ bit))]
            found = found + [mask ^ bit for mask in found]
        parts.append(pieces)
        each = len(found) // 2
        spots.append(
            [
                (2 * other + found.index(mask) // each, found.index(mask) % each)
                for other in range(2)
                for mask in range(chans)
            ]
        )

    gated = convolve(core, gates, filters, skip, direct, crossed, [])

    spread = lax.all_to_all(
        gated.reshape(chans, rows, gated.shape[1]), "chan", split_axis=0, concat_axis=0
    )
    flat = fence([piece for pieces in parts for piece in pieces], [gated])
    swaps = [swap(piece) for piece in flat]
    parts = [[*flat[at : at + 2], *swaps[at : at + 2]] for at in (0, 2)]
    (spread,) = fence([spread], swaps)
    order = [which * chans + (chan ^ mask) for which in (core, 1 - core) for mask in range(chans)]
    acts = part(jnp.stack([*order, pair]).astype(jnp.int32), spread)
    for step in range(1, pairs):
        acts[step] = permute(acts[step], lambda p, k, c, step=step: (p ^ step, k, c))

    count = pairs.bit_length() - 1
    steps = [1 << index for index in range(count)]
    ranks = sorted(range(pairs), key=lambda e: [not e & step for step in steps])
    acts = [acts[rank] for rank in ranks]

    chunks = 4
    cols = model // chunks
    outs = []
    for chunk in range(chunks):
        which = chunk // 2
        send, keep = project(
            acts, [(piece, chunk % 2) for piece in parts[which]], spots[which], own_rows, cols
        )
        for index, step in enumerate(steps):
            got = permute(send, lambda p, k, c, step=step: (p ^ step, k, c)).astype(F32)
            many = got.shape[0] // 2
            if index + 1 < count:
                send = (keep[:many] + got[:many]).astype(BF16)
                keep = keep[many:] + got[many:]
            else:
                keep = keep + got
        outs.append(keep.astype(BF16))
    return jnp.concatenate(outs, axis=1)


def solution(mesh):
    in_specs = (
        P("seq", "chan"),
        P("seq", "chan"),
        P(None, "chan"),
        P("chan"),
        P(("seq", "chan"), None),
    )
    out_specs = P(("seq", "chan"), None)
    return jax.shard_map(body, mesh=mesh, in_specs=in_specs, out_specs=out_specs, check_vma=False)
```

```python
import functools
import math

import jax
import jax.numpy as jnp
import numpy as np
from jax import lax
from jax.experimental import pallas as pl
from jax.experimental.pallas import tpu as pltpu
from jax.sharding import PartitionSpec as P

AXES = ("seq", "chan")
F32 = jnp.float32
BF16 = jnp.bfloat16


def sizes():
    return lax.axis_size("seq") // 2, lax.axis_size("chan")


def place(pairs, chans, pair, core, chan):
    return (pair * 2 + core) * chans + chan


def permute(value, move):
    pairs, chans = sizes()
    route = []
    for pair in range(pairs):
        for core in range(2):
            for chan in range(chans):
                target = move(pair, core, chan)
                if target is not None and 0 <= target[0] < pairs:
                    route.append(
                        (place(pairs, chans, pair, core, chan), place(pairs, chans, *target))
                    )
    return lax.ppermute(value, AXES, route)


def table(block):
    order = np.concatenate([np.arange(0, block, 2), np.arange(1, block, 2)])
    phase = (2 * order[:, None] + 1) * np.arange(block)[None, :] % (4 * block)
    angle = phase * (math.pi / (2 * block))
    return np.concatenate([np.cos(angle), np.sin(angle)], axis=0)


def conv_kernel(lags, core_ref, table_ref, back_ref, skip_ref, gates_ref, filters_ref, *rest):
    block_refs, out_refs = rest[: lags + 2], rest[-2:]
    block = gates_ref.shape[0]
    half = block // 2
    odd = core_ref[0] == 1
    reach = lags // 2

    def transform(operand):
        return jnp.dot(table_ref[...], operand, preferred_element_type=F32)

    direct = block_refs[: reach + 1]
    crossed = block_refs[reach + 1 :]
    cos_parts, sin_parts = [], []
    for lag in range(lags + 1):
        if lag % 2 == 0:
            operand = direct[lag // 2][...]
        else:
            operand = jnp.where(odd, crossed[lag // 2][...], crossed[lag // 2 + 1][...])
        both = transform(operand)
        cos_parts.append(both[:block])
        sin_parts.append(both[block:])
    real = imag = 0.0
    for lag in range(lags):
        both = transform(filters_ref[lag * block : (lag + 1) * block, :])
        tap_cos, tap_sin = both[:block], both[block:]
        near_cos, near_sin = cos_parts[lag], sin_parts[lag]
        far_cos, far_sin = cos_parts[lag + 1], sin_parts[lag + 1]
        window_cos = jnp.concatenate(
            [near_cos[:half] + far_sin[:half], near_cos[half:] - far_sin[half:]], axis=0
        )
        window_sin = jnp.concatenate(
            [near_sin[:half] - far_cos[:half], near_sin[half:] + far_cos[half:]], axis=0
        )
        real = real + tap_cos * window_cos - tap_sin * window_sin
        imag = imag + tap_cos * window_sin + tap_sin * window_cos
    spectrum = jnp.concatenate([real, imag], axis=0).astype(BF16)
    filtered = jnp.dot(back_ref[...], spectrum, preferred_element_type=F32) * (1.0 / block)
    filtered = filtered + skip_ref[...] * direct[0][...].astype(F32)
    result = (gates_ref[...].astype(F32) * filtered).astype(BF16)
    chans, few, _ = out_refs[0].shape
    for chan in range(chans):
        for which, ref in enumerate(out_refs):
            start = (2 * chan + which) * few
            ref[chan] = result[start : start + few]


def convolve(core, gates, filters, skip, direct, crossed, deps):
    block, width = gates.shape
    taps = filters.shape[0]
    lags = taps // block
    forth = table(block)
    _, chans = sizes()
    few = block // chans // 2
    tile = min(width, 512)

    def column(rows):
        return pl.BlockSpec((rows, tile), lambda i, *_: (0, i))

    def whole(rows, cols):
        return pl.BlockSpec((rows, cols), lambda i, *_: (0, 0))

    blocks = [*direct, *crossed]
    return pl.pallas_call(
        functools.partial(conv_kernel, lags),
        grid_spec=pltpu.PrefetchScalarGridSpec(
            num_scalar_prefetch=1,
            grid=(width // tile,),
            in_specs=[
                whole(2 * block, block),
                whole(block, 2 * block),
                column(1),
                column(block),
                column(taps),
                *[column(block) for _ in blocks],
                *[pl.BlockSpec(memory_space=pl.ANY) for _ in deps],
            ],
            out_specs=[pl.BlockSpec((chans, few, tile), lambda i, *_: (0, 0, i))] * 2,
        ),
        out_shape=[jax.ShapeDtypeStruct((chans, few, width), BF16)] * 2,
        cost_estimate=pl.CostEstimate(
            flops=2 * (3 * lags + 3) * 2 * block * block * width,
            bytes_accessed=2 * width * (taps + (len(blocks) + 2) * block),
            transcendentals=0,
        ),
        name="conv",
    )(
        core.reshape(1),
        jnp.asarray(forth, BF16),
        jnp.asarray(forth.T, BF16),
        skip.reshape(1, width),
        gates,
        filters,
        *blocks,
        *deps,
    )


def join_kernel(count, *refs):
    out_ref = refs[-1]
    start = 0
    for ref in refs[:count]:
        out_ref[start : start + ref.shape[0], :] = ref[...]
        start += ref.shape[0]


def join(parts, cols, deps=()):
    rows = sum(array.shape[0] for array, _ in parts)
    return pl.pallas_call(
        functools.partial(join_kernel, len(parts)),
        grid=(1,),
        in_specs=[
            *[
                pl.BlockSpec((array.shape[0], cols), lambda i, index=index: (0, index))
                for array, index in parts
            ],
            *[pl.BlockSpec(memory_space=pl.ANY) for _ in deps],
        ],
        out_specs=pl.BlockSpec((rows, cols), lambda i: (0, 0)),
        out_shape=jax.ShapeDtypeStruct((rows, cols), BF16),
        compiler_params=pltpu.CompilerParams(vmem_limit_bytes=12 * 2**20),
        name="join",
    )(*[array for array, _ in parts], *deps)


def part_kernel(many, slots, order_ref, from_ref, *refs):
    width = from_ref.shape[2] // slots
    for step, ref in enumerate(refs):
        here = order_ref[slots] ^ step
        if width % 128:
            ref[...] = from_ref[here]
            continue
        for slot in range(slots):
            start = pl.multiple_of(order_ref[slot] * width, width)
            ref[:, slot * width : (slot + 1) * width] = from_ref[here, :, pl.ds(start, width)]


def part(order, array):
    many, rows, depth = array.shape
    slots = order.shape[0] - 1
    width = depth // slots
    if width % 128:
        array = jnp.concatenate(
            [
                lax.dynamic_slice_in_dim(array, order[slot] * width, width, axis=2)
                for slot in range(slots)
            ],
            axis=2,
        )
    return list(
        pl.pallas_call(
            functools.partial(part_kernel, many, slots),
            grid_spec=pltpu.PrefetchScalarGridSpec(
                num_scalar_prefetch=1,
                grid=(1,),
                in_specs=[pl.BlockSpec(array.shape, lambda i, *_: (0, 0, 0))],
                out_specs=[pl.BlockSpec((rows, depth), lambda i, *_: (0, 0))] * many,
            ),
            out_shape=[jax.ShapeDtypeStruct((rows, depth), BF16)] * many,
            compiler_params=pltpu.CompilerParams(vmem_limit_bytes=12 * 2**20),
            name="part",
        )(order, array)
    )


def fence_kernel(*refs):
    del refs


def fence(arrays, deps):
    anywhere = pl.BlockSpec(memory_space=pl.ANY)
    return pl.pallas_call(
        fence_kernel,
        in_specs=[anywhere] * (len(arrays) + len(deps)),
        out_specs=[anywhere] * len(arrays),
        out_shape=[jax.ShapeDtypeStruct(array.shape, array.dtype) for array in arrays],
        input_output_aliases={index: index for index in range(len(arrays))},
        compiler_params=pltpu.CompilerParams(vmem_limit_bytes=2**20),
        name="fence",
    )(*arrays, *deps)


def project_kernel(count, firsts, tile, spots, width, *refs):
    act_refs, piece_refs = refs[:count], refs[count:-2]
    send_ref, keep_ref = refs[-2:]
    rows, cols = send_ref.shape
    acts = jnp.concatenate([act[...] for act in act_refs], axis=0)
    for start in range(0, cols, tile):
        weight = jnp.concatenate(
            [
                piece_refs[piece][
                    spot * width : (spot + 1) * width,
                    firsts[piece] * cols + start : firsts[piece] * cols + start + tile,
                ]
                for piece, spot in spots
            ],
            axis=0,
        )
        total = jnp.dot(acts, weight, preferred_element_type=F32)
        send_ref[:, start : start + tile] = total[:rows].astype(BF16)
        keep_ref[:, start : start + tile] = total[rows:]


def project(acts, pieces, spots, width, cols):
    rows, depth = acts[0].shape
    count = rows * len(acts)
    tile = min(cols, 512)
    firsts = [first for _, first in pieces]
    held = pl.BlockSpec(memory_space=pltpu.VMEM)
    return pl.pallas_call(
        functools.partial(project_kernel, len(acts), firsts, tile, spots, width),
        in_specs=[held] * (len(acts) + len(pieces)),
        out_specs=[held] * 2,
        out_shape=[
            jax.ShapeDtypeStruct((count // 2, cols), BF16),
            jax.ShapeDtypeStruct((count // 2, cols), F32),
        ],
        compiler_params=pltpu.CompilerParams(vmem_limit_bytes=16 * 2**20),
        cost_estimate=pl.CostEstimate(
            flops=2 * count * depth * cols,
            bytes_accessed=2 * depth * cols + 6 * count * cols,
            transcendentals=0,
        ),
        name="project",
    )(*acts, *[piece for piece, _ in pieces])


def body(values, gates, filters, skip, out_weight):
    pairs, chans = sizes()
    seq, chan = lax.axis_index("seq"), lax.axis_index("chan")
    pair, core = seq // 2, seq % 2
    block = values.shape[0]
    lags = filters.shape[0] // block
    own_rows, model = out_weight.shape
    half = model // 2
    rows = block // chans

    def swap(array):
        return permute(array, lambda p, k, c: (p, 1 - k, c))

    direct = [values]
    for _ in range(lags // 2):
        direct.append(permute(direct[-1], lambda p, k, c: (p + 1, k, c)))
    crossed = [
        permute(
            held,
            lambda p, k, c, first=index == 0, last=index == lags // 2: None
            if (first and k == 1) or (last and k == 0)
            else (p, 1 - k, c),
        )
        for index, held in enumerate(direct)
    ]

    bits = [1 << index for index in range(chans.bit_length() - 1)]
    parts, spots = [], []
    for which, order in enumerate((bits, bits[::-1])):
        held = join([(out_weight, which)], half, [crossed[0]])
        found = [0]
        for step, bit in enumerate(order):
            if step:
                held = join([(piece, 0) for piece in pieces], half)
            pieces = [held, permute(held, lambda p, k, c, bit=bit: (p, k, c ^ bit))]
            found = found + [mask ^ bit for mask in found]
        parts.append(pieces)
        each = len(found) // 2
        spots.append(
            [
                (2 * other + found.index(mask) // each, found.index(mask) % each)
                for other in range(2)
                for mask in range(chans)
            ]
        )

    gated = convolve(core, gates, filters, skip, direct, crossed, [])

    spreads = [lax.all_to_all(some, "chan", split_axis=0, concat_axis=0) for some in gated]

    flat = fence([piece for pieces in parts for piece in pieces], gated[:1])
    swaps = [swap(piece) for piece in flat]
    parts = [[*flat[at : at + 2], *swaps[at : at + 2]] for at in (0, 2)]
    spreads = [fence([some], swaps)[0] for some in spreads]
    order = [which * chans + (chan ^ mask) for which in (core, 1 - core) for mask in range(chans)]
    order = jnp.stack([*order, pair]).astype(jnp.int32)
    acts = []
    for spread in spreads:
        some = part(order, spread)
        for step in range(1, pairs):
            some[step] = permute(some[step], lambda p, k, c, step=step: (p ^ step, k, c))
        acts.append(some)

    count = pairs.bit_length() - 1
    steps = [1 << index for index in range(count)]
    ranks = sorted(range(pairs), key=lambda e: [not e & step for step in steps])
    acts = [[some[rank] for rank in ranks] for some in acts]

    outs = []
    for some in acts:
        row = []
        for which in range(2):
            send, keep = project(
                some, [(piece, 0) for piece in parts[which]], spots[which], own_rows, half
            )
            for index, step in enumerate(steps):
                got = permute(send, lambda p, k, c, step=step: (p ^ step, k, c)).astype(F32)
                many = got.shape[0] // 2
                if index + 1 < count:
                    send = (keep[:many] + got[:many]).astype(BF16)
                    keep = keep[many:] + got[many:]
                else:
                    keep = keep + got
            row.append(keep.astype(BF16))
        outs.append(jnp.concatenate(row, axis=1))
    return jnp.concatenate(outs, axis=0)


def solution(mesh):
    in_specs = (
        P("seq", "chan"),
        P("seq", "chan"),
        P(None, "chan"),
        P("chan"),
        P(("seq", "chan"), None),
    )
    out_specs = P(("seq", "chan"), None)
    return jax.shard_map(body, mesh=mesh, in_specs=in_specs, out_specs=out_specs, check_vma=False)
```

```python
import functools
import math

import jax
import jax.numpy as jnp
import numpy as np
from jax import lax
from jax.experimental import pallas as pl
from jax.experimental.pallas import tpu as pltpu
from jax.sharding import PartitionSpec as P

AXES = ("seq", "chan")
F32 = jnp.float32
BF16 = jnp.bfloat16


def sizes():
    return lax.axis_size("seq") // 2, lax.axis_size("chan")


def place(pairs, chans, pair, core, chan):
    return (pair * 2 + core) * chans + chan


def permute(value, move):
    pairs, chans = sizes()
    route = []
    for pair in range(pairs):
        for core in range(2):
            for chan in range(chans):
                target = move(pair, core, chan)
                if target is not None and 0 <= target[0] < pairs:
                    route.append(
                        (place(pairs, chans, pair, core, chan), place(pairs, chans, *target))
                    )
    return lax.ppermute(value, AXES, route)


def table(block):
    order = np.concatenate([np.arange(0, block, 2), np.arange(1, block, 2)])
    phase = (2 * order[:, None] + 1) * np.arange(block)[None, :] % (4 * block)
    angle = phase * (math.pi / (2 * block))
    return np.concatenate([np.cos(angle), np.sin(angle)], axis=0)


def conv_kernel(lags, core_ref, table_ref, back_ref, skip_ref, gates_ref, filters_ref, *rest):
    block_refs, out_refs = rest[: lags + 2], rest[-2:]
    block = gates_ref.shape[0]
    half = block // 2
    odd = core_ref[0] == 1
    reach = lags // 2

    def transform(operand):
        return jnp.dot(table_ref[...], operand, preferred_element_type=F32)

    direct = block_refs[: reach + 1]
    crossed = block_refs[reach + 1 :]
    cos_parts, sin_parts = [], []
    for lag in range(lags + 1):
        if lag % 2 == 0:
            operand = direct[lag // 2][...]
        else:
            operand = jnp.where(odd, crossed[lag // 2][...], crossed[lag // 2 + 1][...])
        both = transform(operand)
        cos_parts.append(both[:block])
        sin_parts.append(both[block:])
    real = imag = 0.0
    for lag in range(lags):
        both = transform(filters_ref[lag * block : (lag + 1) * block, :])
        tap_cos, tap_sin = both[:block], both[block:]
        near_cos, near_sin = cos_parts[lag], sin_parts[lag]
        far_cos, far_sin = cos_parts[lag + 1], sin_parts[lag + 1]
        window_cos = jnp.concatenate(
            [near_cos[:half] + far_sin[:half], near_cos[half:] - far_sin[half:]], axis=0
        )
        window_sin = jnp.concatenate(
            [near_sin[:half] - far_cos[:half], near_sin[half:] + far_cos[half:]], axis=0
        )
        real = real + tap_cos * window_cos - tap_sin * window_sin
        imag = imag + tap_cos * window_sin + tap_sin * window_cos
    spectrum = jnp.concatenate([real, imag], axis=0).astype(BF16)
    filtered = jnp.dot(back_ref[...], spectrum, preferred_element_type=F32) * (1.0 / block)
    filtered = filtered + skip_ref[...] * direct[0][...].astype(F32)
    result = (gates_ref[...].astype(F32) * filtered).astype(BF16)
    chans, few, _ = out_refs[0].shape
    for chan in range(chans):
        for which, ref in enumerate(out_refs):
            start = (2 * chan + which) * few
            ref[chan] = result[start : start + few]


def convolve(core, gates, filters, skip, direct, crossed, deps):
    block, width = gates.shape
    taps = filters.shape[0]
    lags = taps // block
    forth = table(block)
    _, chans = sizes()
    few = block // chans // 2
    tile = min(width, 512)

    def column(rows):
        return pl.BlockSpec((rows, tile), lambda i, *_: (0, i))

    def whole(rows, cols):
        return pl.BlockSpec((rows, cols), lambda i, *_: (0, 0))

    blocks = [*direct, *crossed]
    return pl.pallas_call(
        functools.partial(conv_kernel, lags),
        grid_spec=pltpu.PrefetchScalarGridSpec(
            num_scalar_prefetch=1,
            grid=(width // tile,),
            in_specs=[
                whole(2 * block, block),
                whole(block, 2 * block),
                column(1),
                column(block),
                column(taps),
                *[column(block) for _ in blocks],
                *[pl.BlockSpec(memory_space=pl.ANY) for _ in deps],
            ],
            out_specs=[pl.BlockSpec((chans, few, tile), lambda i, *_: (0, 0, i))] * 2,
        ),
        out_shape=[jax.ShapeDtypeStruct((chans, few, width), BF16)] * 2,
        cost_estimate=pl.CostEstimate(
            flops=2 * (3 * lags + 3) * 2 * block * block * width,
            bytes_accessed=2 * width * (taps + (len(blocks) + 2) * block),
            transcendentals=0,
        ),
        name="conv",
    )(
        core.reshape(1),
        jnp.asarray(forth, BF16),
        jnp.asarray(forth.T, BF16),
        skip.reshape(1, width),
        gates,
        filters,
        *blocks,
        *deps,
    )


def join_kernel(count, *refs):
    out_ref = refs[-1]
    start = 0
    for ref in refs[:count]:
        out_ref[start : start + ref.shape[0], :] = ref[...]
        start += ref.shape[0]


def join(parts, cols, deps=()):
    rows = sum(array.shape[0] for array, _ in parts)
    return pl.pallas_call(
        functools.partial(join_kernel, len(parts)),
        grid=(1,),
        in_specs=[
            *[
                pl.BlockSpec((array.shape[0], cols), lambda i, index=index: (0, index))
                for array, index in parts
            ],
            *[pl.BlockSpec(memory_space=pl.ANY) for _ in deps],
        ],
        out_specs=pl.BlockSpec((rows, cols), lambda i: (0, 0)),
        out_shape=jax.ShapeDtypeStruct((rows, cols), BF16),
        compiler_params=pltpu.CompilerParams(vmem_limit_bytes=12 * 2**20),
        name="join",
    )(*[array for array, _ in parts], *deps)


def part_kernel(many, slots, order_ref, from_ref, *refs):
    width = from_ref.shape[2] // slots
    for step, ref in enumerate(refs):
        here = order_ref[slots] ^ step
        if width % 128:
            ref[...] = from_ref[here]
            continue
        for slot in range(slots):
            start = pl.multiple_of(order_ref[slot] * width, width)
            ref[:, slot * width : (slot + 1) * width] = from_ref[here, :, pl.ds(start, width)]


def part(order, array):
    many, rows, depth = array.shape
    slots = order.shape[0] - 1
    width = depth // slots
    if width % 128:
        array = jnp.concatenate(
            [
                lax.dynamic_slice_in_dim(array, order[slot] * width, width, axis=2)
                for slot in range(slots)
            ],
            axis=2,
        )
    return list(
        pl.pallas_call(
            functools.partial(part_kernel, many, slots),
            grid_spec=pltpu.PrefetchScalarGridSpec(
                num_scalar_prefetch=1,
                grid=(1,),
                in_specs=[pl.BlockSpec(array.shape, lambda i, *_: (0, 0, 0))],
                out_specs=[pl.BlockSpec((rows, depth), lambda i, *_: (0, 0))] * many,
            ),
            out_shape=[jax.ShapeDtypeStruct((rows, depth), BF16)] * many,
            compiler_params=pltpu.CompilerParams(vmem_limit_bytes=12 * 2**20),
            name="part",
        )(order, array)
    )


def fence_kernel(*refs):
    del refs


def fence(arrays, deps):
    anywhere = pl.BlockSpec(memory_space=pl.ANY)
    return pl.pallas_call(
        fence_kernel,
        in_specs=[anywhere] * (len(arrays) + len(deps)),
        out_specs=[anywhere] * len(arrays),
        out_shape=[jax.ShapeDtypeStruct(array.shape, array.dtype) for array in arrays],
        input_output_aliases={index: index for index in range(len(arrays))},
        compiler_params=pltpu.CompilerParams(vmem_limit_bytes=2**20),
        name="fence",
    )(*arrays, *deps)


def project_kernel(count, firsts, tile, spots, width, *refs):
    act_refs, piece_refs = refs[:count], refs[count : count + len(firsts)]
    send_ref, keep_ref = refs[-2:]
    rows, cols = send_ref.shape
    acts = jnp.concatenate([act[...] for act in act_refs], axis=0)
    for start in range(0, cols, tile):
        weight = jnp.concatenate(
            [
                piece_refs[piece][
                    spot * width : (spot + 1) * width,
                    firsts[piece] * cols + start : firsts[piece] * cols + start + tile,
                ]
                for piece, spot in spots
            ],
            axis=0,
        )
        total = jnp.dot(acts, weight, preferred_element_type=F32)
        send_ref[:, start : start + tile] = total[:rows].astype(BF16)
        keep_ref[:, start : start + tile] = total[rows:]


def project(acts, pieces, spots, width, cols, deps):
    rows, depth = acts[0].shape
    count = rows * len(acts)
    tile = min(cols, 512)
    firsts = [first for _, first in pieces]
    held = pl.BlockSpec(memory_space=pltpu.VMEM)
    return pl.pallas_call(
        functools.partial(project_kernel, len(acts), firsts, tile, spots, width),
        in_specs=[held] * (len(acts) + len(pieces))
        + [pl.BlockSpec(memory_space=pl.ANY)] * len(deps),
        out_specs=[held] * 2,
        out_shape=[
            jax.ShapeDtypeStruct((count // 2, cols), BF16),
            jax.ShapeDtypeStruct((count // 2, cols), F32),
        ],
        compiler_params=pltpu.CompilerParams(vmem_limit_bytes=16 * 2**20),
        cost_estimate=pl.CostEstimate(
            flops=2 * count * depth * cols,
            bytes_accessed=2 * depth * cols + 6 * count * cols,
            transcendentals=0,
        ),
        name="project",
    )(*acts, *[piece for piece, _ in pieces], *deps)


def body(values, gates, filters, skip, out_weight):
    pairs, chans = sizes()
    seq, chan = lax.axis_index("seq"), lax.axis_index("chan")
    pair, core = seq // 2, seq % 2
    block = values.shape[0]
    lags = filters.shape[0] // block
    own_rows, model = out_weight.shape
    half = model // 2
    rows = block // chans

    def swap(array):
        return permute(array, lambda p, k, c: (p, 1 - k, c))

    direct = [values]
    for _ in range(lags // 2):
        direct.append(permute(direct[-1], lambda p, k, c: (p + 1, k, c)))
    crossed = [
        permute(
            held,
            lambda p, k, c, first=index == 0, last=index == lags // 2: None
            if (first and k == 1) or (last and k == 0)
            else (p, 1 - k, c),
        )
        for index, held in enumerate(direct)
    ]

    bits = [1 << index for index in range(chans.bit_length() - 1)]
    parts, spots = [], []
    for which, order in enumerate((bits, bits[::-1])):
        held = join([(out_weight, which)], half, [crossed[0]])
        found = [0]
        for step, bit in enumerate(order):
            if step:
                held = join([(piece, 0) for piece in pieces], half)
            pieces = [held, permute(held, lambda p, k, c, bit=bit: (p, k, c ^ bit))]
            found = found + [mask ^ bit for mask in found]
        parts.append(pieces)
        each = len(found) // 2
        spots.append(
            [
                (2 * other + found.index(mask) // each, found.index(mask) % each)
                for other in range(2)
                for mask in range(chans)
            ]
        )

    gated = convolve(core, gates, filters, skip, direct, crossed, [])

    spreads = [lax.all_to_all(some, "chan", split_axis=0, concat_axis=0) for some in gated]

    flat = fence([piece for pieces in parts for piece in pieces], gated[:1])
    swaps = [swap(piece) for piece in flat]
    parts = [[*flat[at : at + 2], *swaps[at : at + 2]] for at in (0, 2)]
    spreads = [fence([some], swaps)[0] for some in spreads]
    order = [which * chans + (chan ^ mask) for which in (core, 1 - core) for mask in range(chans)]
    order = jnp.stack([*order, pair]).astype(jnp.int32)
    acts = []
    for spread in spreads:
        some = part(order, spread)
        for step in range(1, pairs):
            some[step] = permute(some[step], lambda p, k, c, step=step: (p ^ step, k, c))
        acts.append(some)

    count = pairs.bit_length() - 1
    steps = [1 << index for index in range(count)]
    ranks = sorted(range(pairs), key=lambda e: [not e & step for step in steps])
    acts = [[some[rank] for rank in ranks] for some in acts]

    outs = []
    passed = []
    for some in acts:
        row, sent = [], []
        for which in range(2):
            send, keep = project(
                some,
                [(piece, 0) for piece in parts[which]],
                spots[which],
                own_rows,
                half,
                passed[:1] if which == 0 else [],
            )
            for index, step in enumerate(steps):
                got = permute(send, lambda p, k, c, step=step: (p ^ step, k, c)).astype(F32)
                many = got.shape[0] // 2
                if index + 1 < count:
                    send = (keep[:many] + got[:many]).astype(BF16)
                    sent.append(send)
                    keep = keep[many:] + got[many:]
                else:
                    keep = keep + got
            row.append(keep.astype(BF16))
        passed = sent
        outs.append(jnp.concatenate(row, axis=1))
    return jnp.concatenate(outs, axis=0)


def solution(mesh):
    in_specs = (
        P("seq", "chan"),
        P("seq", "chan"),
        P(None, "chan"),
        P("chan"),
        P(("seq", "chan"), None),
    )
    out_specs = P(("seq", "chan"), None)
    return jax.shard_map(body, mesh=mesh, in_specs=in_specs, out_specs=out_specs, check_vma=False)
```

```python
import functools
import math

import jax
import jax.numpy as jnp
import numpy as np
from jax import lax
from jax.experimental import pallas as pl
from jax.experimental.pallas import tpu as pltpu
from jax.sharding import PartitionSpec as P

AXES = ("seq", "chan")
F32 = jnp.float32
BF16 = jnp.bfloat16


def sizes():
    return lax.axis_size("seq") // 2, lax.axis_size("chan")


def place(pairs, chans, pair, core, chan):
    return (pair * 2 + core) * chans + chan


def permute(value, move):
    pairs, chans = sizes()
    route = []
    for pair in range(pairs):
        for core in range(2):
            for chan in range(chans):
                target = move(pair, core, chan)
                if target is not None and 0 <= target[0] < pairs:
                    route.append(
                        (place(pairs, chans, pair, core, chan), place(pairs, chans, *target))
                    )
    return lax.ppermute(value, AXES, route)


def table(block):
    order = np.concatenate([np.arange(0, block, 2), np.arange(1, block, 2)])
    phase = (2 * order[:, None] + 1) * np.arange(block)[None, :] % (4 * block)
    angle = phase * (math.pi / (2 * block))
    return np.concatenate([np.cos(angle), np.sin(angle)], axis=0)


def conv_kernel(lags, core_ref, table_ref, back_ref, skip_ref, gates_ref, filters_ref, *rest):
    block_refs, out_refs = rest[: lags + 2], rest[-2:]
    block = gates_ref.shape[0]
    half = block // 2
    odd = core_ref[0] == 1
    reach = lags // 2

    def transform(operand):
        return jnp.dot(table_ref[...], operand, preferred_element_type=F32)

    direct = block_refs[: reach + 1]
    crossed = block_refs[reach + 1 :]
    cos_parts, sin_parts = [], []
    for lag in range(lags + 1):
        if lag % 2 == 0:
            operand = direct[lag // 2][...]
        else:
            operand = jnp.where(odd, crossed[lag // 2][...], crossed[lag // 2 + 1][...])
        both = transform(operand)
        cos_parts.append(both[:block])
        sin_parts.append(both[block:])
    real = imag = 0.0
    for lag in range(lags):
        both = transform(filters_ref[lag * block : (lag + 1) * block, :])
        tap_cos, tap_sin = both[:block], both[block:]
        near_cos, near_sin = cos_parts[lag], sin_parts[lag]
        far_cos, far_sin = cos_parts[lag + 1], sin_parts[lag + 1]
        window_cos = jnp.concatenate(
            [near_cos[:half] + far_sin[:half], near_cos[half:] - far_sin[half:]], axis=0
        )
        window_sin = jnp.concatenate(
            [near_sin[:half] - far_cos[:half], near_sin[half:] + far_cos[half:]], axis=0
        )
        real = real + tap_cos * window_cos - tap_sin * window_sin
        imag = imag + tap_cos * window_sin + tap_sin * window_cos
    spectrum = jnp.concatenate([real, imag], axis=0).astype(BF16)
    filtered = jnp.dot(back_ref[...], spectrum, preferred_element_type=F32) * (1.0 / block)
    filtered = filtered + skip_ref[...] * direct[0][...].astype(F32)
    result = (gates_ref[...].astype(F32) * filtered).astype(BF16)
    chans, few, _ = out_refs[0].shape
    for chan in range(chans):
        for which, ref in enumerate(out_refs):
            start = (2 * chan + which) * few
            ref[chan] = result[start : start + few]


def convolve(core, gates, filters, skip, direct, crossed, deps):
    block, width = gates.shape
    taps = filters.shape[0]
    lags = taps // block
    forth = table(block)
    _, chans = sizes()
    few = block // chans // 2
    tile = min(width, 512)

    def column(rows):
        return pl.BlockSpec((rows, tile), lambda i, *_: (0, i))

    def whole(rows, cols):
        return pl.BlockSpec((rows, cols), lambda i, *_: (0, 0))

    blocks = [*direct, *crossed]
    return pl.pallas_call(
        functools.partial(conv_kernel, lags),
        grid_spec=pltpu.PrefetchScalarGridSpec(
            num_scalar_prefetch=1,
            grid=(width // tile,),
            in_specs=[
                whole(2 * block, block),
                whole(block, 2 * block),
                column(1),
                column(block),
                column(taps),
                *[column(block) for _ in blocks],
                *[pl.BlockSpec(memory_space=pl.ANY) for _ in deps],
            ],
            out_specs=[pl.BlockSpec((chans, few, tile), lambda i, *_: (0, 0, i))] * 2,
        ),
        out_shape=[jax.ShapeDtypeStruct((chans, few, width), BF16)] * 2,
        cost_estimate=pl.CostEstimate(
            flops=2 * (3 * lags + 3) * 2 * block * block * width,
            bytes_accessed=2 * width * (taps + (len(blocks) + 2) * block),
            transcendentals=0,
        ),
        name="conv",
    )(
        core.reshape(1),
        jnp.asarray(forth, BF16),
        jnp.asarray(forth.T, BF16),
        skip.reshape(1, width),
        gates,
        filters,
        *blocks,
        *deps,
    )


def join_kernel(count, *refs):
    out_ref = refs[-1]
    start = 0
    for ref in refs[:count]:
        out_ref[start : start + ref.shape[0], :] = ref[...]
        start += ref.shape[0]


def join(parts, cols, deps=()):
    rows = sum(array.shape[0] for array, _ in parts)
    return pl.pallas_call(
        functools.partial(join_kernel, len(parts)),
        grid=(1,),
        in_specs=[
            *[
                pl.BlockSpec((array.shape[0], cols), lambda i, index=index: (0, index))
                for array, index in parts
            ],
            *[pl.BlockSpec(memory_space=pl.ANY) for _ in deps],
        ],
        out_specs=pl.BlockSpec((rows, cols), lambda i: (0, 0)),
        out_shape=jax.ShapeDtypeStruct((rows, cols), BF16),
        compiler_params=pltpu.CompilerParams(vmem_limit_bytes=12 * 2**20),
        name="join",
    )(*[array for array, _ in parts], *deps)


def part_kernel(many, slots, order_ref, from_ref, *refs):
    width = from_ref.shape[2] // slots
    for step, ref in enumerate(refs):
        here = order_ref[slots] ^ step
        if width % 128:
            ref[...] = from_ref[here]
            continue
        for slot in range(slots):
            start = pl.multiple_of(order_ref[slot] * width, width)
            ref[:, slot * width : (slot + 1) * width] = from_ref[here, :, pl.ds(start, width)]


def part(order, array):
    many, rows, depth = array.shape
    slots = order.shape[0] - 1
    width = depth // slots
    if width % 128:
        array = jnp.concatenate(
            [
                lax.dynamic_slice_in_dim(array, order[slot] * width, width, axis=2)
                for slot in range(slots)
            ],
            axis=2,
        )
    return list(
        pl.pallas_call(
            functools.partial(part_kernel, many, slots),
            grid_spec=pltpu.PrefetchScalarGridSpec(
                num_scalar_prefetch=1,
                grid=(1,),
                in_specs=[pl.BlockSpec(array.shape, lambda i, *_: (0, 0, 0))],
                out_specs=[pl.BlockSpec((rows, depth), lambda i, *_: (0, 0))] * many,
            ),
            out_shape=[jax.ShapeDtypeStruct((rows, depth), BF16)] * many,
            compiler_params=pltpu.CompilerParams(vmem_limit_bytes=12 * 2**20),
            name="part",
        )(order, array)
    )


def fence_kernel(*refs):
    del refs


def fence(arrays, deps):
    anywhere = pl.BlockSpec(memory_space=pl.ANY)
    return pl.pallas_call(
        fence_kernel,
        in_specs=[anywhere] * (len(arrays) + len(deps)),
        out_specs=[anywhere] * len(arrays),
        out_shape=[jax.ShapeDtypeStruct(array.shape, array.dtype) for array in arrays],
        input_output_aliases={index: index for index in range(len(arrays))},
        compiler_params=pltpu.CompilerParams(vmem_limit_bytes=2**20),
        name="fence",
    )(*arrays, *deps)


def project_kernel(count, firsts, tile, spots, width, *refs):
    act_refs, piece_refs = refs[:count], refs[count : count + len(firsts)]
    send_ref, keep_ref = refs[-2:]
    rows, cols = send_ref.shape
    acts = jnp.concatenate([act[...] for act in act_refs], axis=0)
    for start in range(0, cols, tile):
        weight = jnp.concatenate(
            [
                piece_refs[piece][
                    spot * width : (spot + 1) * width,
                    firsts[piece] * cols + start : firsts[piece] * cols + start + tile,
                ]
                for piece, spot in spots
            ],
            axis=0,
        )
        total = jnp.dot(acts, weight, preferred_element_type=F32)
        send_ref[:, start : start + tile] = total[:rows].astype(BF16)
        keep_ref[:, start : start + tile] = total[rows:]


def project(acts, pieces, spots, width, cols, deps):
    rows, depth = acts[0].shape
    count = rows * len(acts)
    tile = min(cols, 512)
    firsts = [first for _, first in pieces]
    held = pl.BlockSpec(memory_space=pltpu.VMEM)
    return pl.pallas_call(
        functools.partial(project_kernel, len(acts), firsts, tile, spots, width),
        in_specs=[held] * (len(acts) + len(pieces))
        + [pl.BlockSpec(memory_space=pl.ANY)] * len(deps),
        out_specs=[held] * 2,
        out_shape=[
            jax.ShapeDtypeStruct((count // 2, cols), BF16),
            jax.ShapeDtypeStruct((count // 2, cols), F32),
        ],
        compiler_params=pltpu.CompilerParams(vmem_limit_bytes=16 * 2**20),
        cost_estimate=pl.CostEstimate(
            flops=2 * count * depth * cols,
            bytes_accessed=2 * depth * cols + 6 * count * cols,
            transcendentals=0,
        ),
        name="project",
    )(*acts, *[piece for piece, _ in pieces], *deps)


def body(values, gates, filters, skip, out_weight):
    pairs, chans = sizes()
    seq, chan = lax.axis_index("seq"), lax.axis_index("chan")
    pair, core = seq // 2, seq % 2
    block = values.shape[0]
    lags = filters.shape[0] // block
    own_rows, model = out_weight.shape
    half = model // 2
    rows = block // chans

    def swap(array):
        return permute(array, lambda p, k, c: (p, 1 - k, c))

    direct = [values]
    for _ in range(lags // 2):
        direct.append(permute(direct[-1], lambda p, k, c: (p + 1, k, c)))
    crossed = [
        permute(
            held,
            lambda p, k, c, first=index == 0, last=index == lags // 2: None
            if (first and k == 1) or (last and k == 0)
            else (p, 1 - k, c),
        )
        for index, held in enumerate(direct)
    ]

    bits = [1 << index for index in range(chans.bit_length() - 1)]
    parts, spots = [], []
    for which, order in enumerate((bits, bits[::-1])):
        held = join([(out_weight, which)], half)
        found = [0]
        for step, bit in enumerate(order):
            if step:
                held = join([(piece, 0) for piece in pieces], half)
            pieces = [held, permute(held, lambda p, k, c, bit=bit: (p, k, c ^ bit))]
            found = found + [mask ^ bit for mask in found]
        parts.append(pieces)
        each = len(found) // 2
        spots.append(
            [
                (2 * other + found.index(mask) // each, found.index(mask) % each)
                for other in range(2)
                for mask in range(chans)
            ]
        )

    gated = convolve(core, gates, filters, skip, direct, crossed, [])

    spreads = [lax.all_to_all(some, "chan", split_axis=0, concat_axis=0) for some in gated]

    flat = fence([piece for pieces in parts for piece in pieces], gated[:1])
    swaps = [swap(piece) for piece in flat]
    parts = [[*flat[at : at + 2], *swaps[at : at + 2]] for at in (0, 2)]
    spreads = [fence([some], swaps)[0] for some in spreads]
    order = [which * chans + (chan ^ mask) for which in (core, 1 - core) for mask in range(chans)]
    order = jnp.stack([*order, pair]).astype(jnp.int32)
    acts = []
    for spread in spreads:
        some = part(order, spread)
        for step in range(1, pairs):
            some[step] = permute(some[step], lambda p, k, c, step=step: (p ^ step, k, c))
        acts.append(some)

    count = pairs.bit_length() - 1
    steps = [1 << index for index in range(count)]
    ranks = sorted(range(pairs), key=lambda e: [not e & step for step in steps])
    acts = [[some[rank] for rank in ranks] for some in acts]

    outs = []
    passed = []
    for some in acts:
        row, sent = [], []
        for which in range(2):
            send, keep = project(
                some,
                [(piece, 0) for piece in parts[which]],
                spots[which],
                own_rows,
                half,
                passed[:1] if which == 0 else [],
            )
            for index, step in enumerate(steps):
                got = permute(send, lambda p, k, c, step=step: (p ^ step, k, c)).astype(F32)
                many = got.shape[0] // 2
                if index + 1 < count:
                    send = (keep[:many] + got[:many]).astype(BF16)
                    sent.append(send)
                    keep = keep[many:] + got[many:]
                else:
                    keep = keep + got
            row.append(keep.astype(BF16))
        passed = sent
        outs.append(jnp.concatenate(row, axis=1))
    return jnp.concatenate(outs, axis=0)


def solution(mesh):
    in_specs = (
        P("seq", "chan"),
        P("seq", "chan"),
        P(None, "chan"),
        P("chan"),
        P(("seq", "chan"), None),
    )
    out_specs = P(("seq", "chan"), None)
    return jax.shard_map(body, mesh=mesh, in_specs=in_specs, out_specs=out_specs, check_vma=False)
```

```python
import functools
import math

import jax
import jax.numpy as jnp
import numpy as np
from jax import lax
from jax.experimental import pallas as pl
from jax.experimental.pallas import tpu as pltpu
from jax.sharding import PartitionSpec as P

AXES = ("seq", "chan")
F32 = jnp.float32
BF16 = jnp.bfloat16


def sizes():
    return lax.axis_size("seq") // 2, lax.axis_size("chan")


def place(pairs, chans, pair, core, chan):
    return (pair * 2 + core) * chans + chan


def permute(value, move):
    pairs, chans = sizes()
    route = []
    for pair in range(pairs):
        for core in range(2):
            for chan in range(chans):
                target = move(pair, core, chan)
                if target is not None and 0 <= target[0] < pairs:
                    route.append(
                        (place(pairs, chans, pair, core, chan), place(pairs, chans, *target))
                    )
    return lax.ppermute(value, AXES, route)


def table(block):
    order = np.concatenate([np.arange(0, block, 2), np.arange(1, block, 2)])
    phase = (2 * order[:, None] + 1) * np.arange(block)[None, :] % (4 * block)
    angle = phase * (math.pi / (2 * block))
    return np.concatenate([np.cos(angle), np.sin(angle)], axis=0)


def conv_kernel(lags, core_ref, table_ref, back_ref, skip_ref, gates_ref, filters_ref, *rest):
    block_refs, out_refs = rest[: lags + 2], rest[-2:]
    block = gates_ref.shape[0]
    half = block // 2
    odd = core_ref[0] == 1
    reach = lags // 2

    def transform(operand):
        return jnp.dot(table_ref[...], operand, preferred_element_type=F32)

    direct = block_refs[: reach + 1]
    crossed = block_refs[reach + 1 :]
    cos_parts, sin_parts = [], []
    for lag in range(lags + 1):
        if lag % 2 == 0:
            operand = direct[lag // 2][...]
        else:
            operand = jnp.where(odd, crossed[lag // 2][...], crossed[lag // 2 + 1][...])
        both = transform(operand)
        cos_parts.append(both[:block])
        sin_parts.append(both[block:])
    real = imag = 0.0
    for lag in range(lags):
        both = transform(filters_ref[lag * block : (lag + 1) * block, :])
        tap_cos, tap_sin = both[:block], both[block:]
        near_cos, near_sin = cos_parts[lag], sin_parts[lag]
        far_cos, far_sin = cos_parts[lag + 1], sin_parts[lag + 1]
        window_cos = jnp.concatenate(
            [near_cos[:half] + far_sin[:half], near_cos[half:] - far_sin[half:]], axis=0
        )
        window_sin = jnp.concatenate(
            [near_sin[:half] - far_cos[:half], near_sin[half:] + far_cos[half:]], axis=0
        )
        real = real + tap_cos * window_cos - tap_sin * window_sin
        imag = imag + tap_cos * window_sin + tap_sin * window_cos
    spectrum = jnp.concatenate([real, imag], axis=0).astype(BF16)
    filtered = jnp.dot(back_ref[...], spectrum, preferred_element_type=F32) * (1.0 / block)
    filtered = filtered + skip_ref[...] * direct[0][...].astype(F32)
    result = (gates_ref[...].astype(F32) * filtered).astype(BF16)
    chans, few, _ = out_refs[0].shape
    for chan in range(chans):
        for which, ref in enumerate(out_refs):
            start = (2 * chan + which) * few
            ref[chan] = result[start : start + few]


def convolve(core, gates, filters, skip, direct, crossed, deps):
    block, width = gates.shape
    taps = filters.shape[0]
    lags = taps // block
    forth = table(block)
    _, chans = sizes()
    few = block // chans // 2
    tile = min(width, 512)

    def column(rows):
        return pl.BlockSpec((rows, tile), lambda i, *_: (0, i))

    def whole(rows, cols):
        return pl.BlockSpec((rows, cols), lambda i, *_: (0, 0))

    blocks = [*direct, *crossed]
    return pl.pallas_call(
        functools.partial(conv_kernel, lags),
        grid_spec=pltpu.PrefetchScalarGridSpec(
            num_scalar_prefetch=1,
            grid=(width // tile,),
            in_specs=[
                whole(2 * block, block),
                whole(block, 2 * block),
                column(1),
                column(block),
                column(taps),
                *[column(block) for _ in blocks],
                *[pl.BlockSpec(memory_space=pl.ANY) for _ in deps],
            ],
            out_specs=[pl.BlockSpec((chans, few, tile), lambda i, *_: (0, 0, i))] * 2,
        ),
        out_shape=[jax.ShapeDtypeStruct((chans, few, width), BF16)] * 2,
        cost_estimate=pl.CostEstimate(
            flops=2 * (3 * lags + 3) * 2 * block * block * width,
            bytes_accessed=2 * width * (taps + (len(blocks) + 2) * block),
            transcendentals=0,
        ),
        name="conv",
    )(
        core.reshape(1),
        jnp.asarray(forth, BF16),
        jnp.asarray(forth.T, BF16),
        skip.reshape(1, width),
        gates,
        filters,
        *blocks,
        *deps,
    )


def join_kernel(count, *refs):
    out_ref = refs[-1]
    start = 0
    for ref in refs[:count]:
        out_ref[start : start + ref.shape[0], :] = ref[...]
        start += ref.shape[0]


def join(parts, cols, deps=()):
    rows = sum(array.shape[0] for array, _ in parts)
    return pl.pallas_call(
        functools.partial(join_kernel, len(parts)),
        grid=(1,),
        in_specs=[
            *[
                pl.BlockSpec((array.shape[0], cols), lambda i, index=index: (0, index))
                for array, index in parts
            ],
            *[pl.BlockSpec(memory_space=pl.ANY) for _ in deps],
        ],
        out_specs=pl.BlockSpec((rows, cols), lambda i: (0, 0)),
        out_shape=jax.ShapeDtypeStruct((rows, cols), BF16),
        compiler_params=pltpu.CompilerParams(vmem_limit_bytes=12 * 2**20),
        name="join",
    )(*[array for array, _ in parts], *deps)


def part_kernel(many, slots, order_ref, from_ref, *refs):
    width = from_ref.shape[2] // slots
    for step, ref in enumerate(refs):
        here = order_ref[slots] ^ step
        if width % 128:
            ref[...] = from_ref[here]
            continue
        for slot in range(slots):
            start = pl.multiple_of(order_ref[slot] * width, width)
            ref[:, slot * width : (slot + 1) * width] = from_ref[here, :, pl.ds(start, width)]


def part(order, array):
    many, rows, depth = array.shape
    slots = order.shape[0] - 1
    width = depth // slots
    if width % 128:
        array = jnp.concatenate(
            [
                lax.dynamic_slice_in_dim(array, order[slot] * width, width, axis=2)
                for slot in range(slots)
            ],
            axis=2,
        )
    return list(
        pl.pallas_call(
            functools.partial(part_kernel, many, slots),
            grid_spec=pltpu.PrefetchScalarGridSpec(
                num_scalar_prefetch=1,
                grid=(1,),
                in_specs=[pl.BlockSpec(array.shape, lambda i, *_: (0, 0, 0))],
                out_specs=[pl.BlockSpec((rows, depth), lambda i, *_: (0, 0))] * many,
            ),
            out_shape=[jax.ShapeDtypeStruct((rows, depth), BF16)] * many,
            compiler_params=pltpu.CompilerParams(vmem_limit_bytes=12 * 2**20),
            name="part",
        )(order, array)
    )


def fence_kernel(*refs):
    del refs


def fence(arrays, deps):
    anywhere = pl.BlockSpec(memory_space=pl.ANY)
    return pl.pallas_call(
        fence_kernel,
        in_specs=[anywhere] * (len(arrays) + len(deps)),
        out_specs=[anywhere] * len(arrays),
        out_shape=[jax.ShapeDtypeStruct(array.shape, array.dtype) for array in arrays],
        input_output_aliases={index: index for index in range(len(arrays))},
        compiler_params=pltpu.CompilerParams(vmem_limit_bytes=2**20),
        name="fence",
    )(*arrays, *deps)


def project_kernel(count, firsts, tile, spots, width, *refs):
    act_refs, piece_refs = refs[:count], refs[count : count + len(firsts)]
    send_ref, keep_ref = refs[-2:]
    rows, cols = send_ref.shape
    acts = jnp.concatenate([act[...] for act in act_refs], axis=0)
    for start in range(0, cols, tile):
        weight = jnp.concatenate(
            [
                piece_refs[piece][
                    spot * width : (spot + 1) * width,
                    firsts[piece] * cols + start : firsts[piece] * cols + start + tile,
                ]
                for piece, spot in spots
            ],
            axis=0,
        )
        total = jnp.dot(acts, weight, preferred_element_type=F32)
        send_ref[:, start : start + tile] = total[:rows].astype(BF16)
        keep_ref[:, start : start + tile] = total[rows:]


def project(acts, pieces, spots, width, cols, deps):
    rows, depth = acts[0].shape
    count = rows * len(acts)
    tile = min(cols, 512)
    firsts = [first for _, first in pieces]
    held = pl.BlockSpec(memory_space=pltpu.VMEM)
    return pl.pallas_call(
        functools.partial(project_kernel, len(acts), firsts, tile, spots, width),
        in_specs=[held] * (len(acts) + len(pieces))
        + [pl.BlockSpec(memory_space=pl.ANY)] * len(deps),
        out_specs=[held] * 2,
        out_shape=[
            jax.ShapeDtypeStruct((count // 2, cols), BF16),
            jax.ShapeDtypeStruct((count // 2, cols), F32),
        ],
        compiler_params=pltpu.CompilerParams(vmem_limit_bytes=16 * 2**20),
        cost_estimate=pl.CostEstimate(
            flops=2 * count * depth * cols,
            bytes_accessed=2 * depth * cols + 6 * count * cols,
            transcendentals=0,
        ),
        name="project",
    )(*acts, *[piece for piece, _ in pieces], *deps)


def body(values, gates, filters, skip, out_weight):
    pairs, chans = sizes()
    seq, chan = lax.axis_index("seq"), lax.axis_index("chan")
    pair, core = seq // 2, seq % 2
    block = values.shape[0]
    lags = filters.shape[0] // block
    own_rows, model = out_weight.shape
    half = model // 2
    rows = block // chans

    def swap(array):
        return permute(array, lambda p, k, c: (p, 1 - k, c))

    direct = [values]
    for _ in range(lags // 2):
        direct.append(permute(direct[-1], lambda p, k, c: (p + 1, k, c)))
    crossed = [
        permute(
            held,
            lambda p, k, c, first=index == 0, last=index == lags // 2: None
            if (first and k == 1) or (last and k == 0)
            else (p, 1 - k, c),
        )
        for index, held in enumerate(direct)
    ]

    bits = [1 << index for index in range(chans.bit_length() - 1)]
    parts, spots = [], []
    for which, order in enumerate((bits, bits[::-1])):
        held = join([(out_weight, which)], half)
        found = [0]
        for step, bit in enumerate(order):
            if step:
                held = join([(piece, 0) for piece in pieces], half)
            pieces = [held, permute(held, lambda p, k, c, bit=bit: (p, k, c ^ bit))]
            found = found + [mask ^ bit for mask in found]
        parts.append(pieces)
        each = len(found) // 2
        spots.append(
            [
                (2 * other + found.index(mask) // each, found.index(mask) % each)
                for other in range(2)
                for mask in range(chans)
            ]
        )

    gated = convolve(core, gates, filters, skip, direct, crossed, [])

    spreads = [lax.all_to_all(some, "chan", split_axis=0, concat_axis=0) for some in gated]

    flat = fence([piece for pieces in parts for piece in pieces], gated[:1])
    swaps = [swap(piece) for piece in flat]
    parts = [[*flat[at : at + 2], *swaps[at : at + 2]] for at in (0, 2)]
    spreads = [fence([some], swaps)[0] for some in spreads]
    order = [which * chans + (chan ^ mask) for which in (core, 1 - core) for mask in range(chans)]
    order = jnp.stack([*order, pair]).astype(jnp.int32)
    acts = []
    for spread in spreads:
        some = part(order, spread)
        for step in range(1, pairs):
            some[step] = permute(some[step], lambda p, k, c, step=step: (p ^ step, k, c))
        acts.append(some)

    count = pairs.bit_length() - 1
    steps = [1 << index for index in range(count)]
    ranks = sorted(range(pairs), key=lambda e: [not e & step for step in steps])
    acts = [[some[rank] for rank in ranks] for some in acts]

    outs = []
    passed = []
    for turn, some in enumerate(acts):
        row, sent = [], []
        for which in range(2):
            chunks = 2 if turn == 1 and which == 0 else 1
            for chunk in range(chunks):
                send, keep = project(
                    some,
                    [(piece, chunk) for piece in parts[which]],
                    spots[which],
                    own_rows,
                    half // chunks,
                    passed[:1] if which == 0 else [],
                )
                for index, step in enumerate(steps):
                    got = permute(send, lambda p, k, c, step=step: (p ^ step, k, c)).astype(F32)
                    many = got.shape[0] // 2
                    if index + 1 < count:
                        send = (keep[:many] + got[:many]).astype(BF16)
                        sent.append(send)
                        keep = keep[many:] + got[many:]
                    else:
                        keep = keep + got
                row.append(keep.astype(BF16))
        passed = sent
        outs.append(jnp.concatenate(row, axis=1))
    return jnp.concatenate(outs, axis=0)


def solution(mesh):
    in_specs = (
        P("seq", "chan"),
        P("seq", "chan"),
        P(None, "chan"),
        P("chan"),
        P(("seq", "chan"), None),
    )
    out_specs = P(("seq", "chan"), None)
    return jax.shard_map(body, mesh=mesh, in_specs=in_specs, out_specs=out_specs, check_vma=False)
```

```python
import functools
import math

import jax
import jax.numpy as jnp
import numpy as np
from jax import lax
from jax.experimental import pallas as pl
from jax.experimental.pallas import tpu as pltpu
from jax.sharding import PartitionSpec as P

AXES = ("seq", "chan")
F32 = jnp.float32
BF16 = jnp.bfloat16


def sizes():
    return lax.axis_size("seq") // 2, lax.axis_size("chan")


def place(pairs, chans, pair, core, chan):
    return (pair * 2 + core) * chans + chan


def permute(value, move):
    pairs, chans = sizes()
    route = []
    for pair in range(pairs):
        for core in range(2):
            for chan in range(chans):
                target = move(pair, core, chan)
                if target is not None and 0 <= target[0] < pairs:
                    route.append(
                        (place(pairs, chans, pair, core, chan), place(pairs, chans, *target))
                    )
    return lax.ppermute(value, AXES, route)


def table(block):
    order = np.concatenate([np.arange(0, block, 2), np.arange(1, block, 2)])
    phase = (2 * order[:, None] + 1) * np.arange(block)[None, :] % (4 * block)
    angle = phase * (math.pi / (2 * block))
    return np.concatenate([np.cos(angle), np.sin(angle)], axis=0)


def conv_kernel(lags, core_ref, table_ref, back_ref, skip_ref, gates_ref, filters_ref, *rest):
    block_refs, out_refs = rest[: lags + 2], rest[-2:]
    block = gates_ref.shape[0]
    half = block // 2
    odd = core_ref[0] == 1
    reach = lags // 2

    def transform(operand):
        return jnp.dot(table_ref[...], operand, preferred_element_type=F32)

    direct = block_refs[: reach + 1]
    crossed = block_refs[reach + 1 :]
    cos_parts, sin_parts = [], []
    for lag in range(lags + 1):
        if lag % 2 == 0:
            operand = direct[lag // 2][...]
        else:
            operand = jnp.where(odd, crossed[lag // 2][...], crossed[lag // 2 + 1][...])
        both = transform(operand)
        cos_parts.append(both[:block])
        sin_parts.append(both[block:])
    real = imag = 0.0
    for lag in range(lags):
        both = transform(filters_ref[lag * block : (lag + 1) * block, :])
        tap_cos, tap_sin = both[:block], both[block:]
        near_cos, near_sin = cos_parts[lag], sin_parts[lag]
        far_cos, far_sin = cos_parts[lag + 1], sin_parts[lag + 1]
        window_cos = jnp.concatenate(
            [near_cos[:half] + far_sin[:half], near_cos[half:] - far_sin[half:]], axis=0
        )
        window_sin = jnp.concatenate(
            [near_sin[:half] - far_cos[:half], near_sin[half:] + far_cos[half:]], axis=0
        )
        real = real + tap_cos * window_cos - tap_sin * window_sin
        imag = imag + tap_cos * window_sin + tap_sin * window_cos
    spectrum = jnp.concatenate([real, imag], axis=0).astype(BF16)
    filtered = jnp.dot(back_ref[...], spectrum, preferred_element_type=F32) * (1.0 / block)
    filtered = filtered + skip_ref[...] * direct[0][...].astype(F32)
    result = (gates_ref[...].astype(F32) * filtered).astype(BF16)
    chans, few, _ = out_refs[0].shape
    for chan in range(chans):
        for which, ref in enumerate(out_refs):
            start = (2 * chan + which) * few
            ref[chan] = result[start : start + few]


def convolve(core, gates, filters, skip, direct, crossed, deps):
    block, width = gates.shape
    taps = filters.shape[0]
    lags = taps // block
    forth = table(block)
    _, chans = sizes()
    few = block // chans // 2
    tile = min(width, 512)

    def column(rows):
        return pl.BlockSpec((rows, tile), lambda i, *_: (0, i))

    def whole(rows, cols):
        return pl.BlockSpec((rows, cols), lambda i, *_: (0, 0))

    blocks = [*direct, *crossed]
    return pl.pallas_call(
        functools.partial(conv_kernel, lags),
        grid_spec=pltpu.PrefetchScalarGridSpec(
            num_scalar_prefetch=1,
            grid=(width // tile,),
            in_specs=[
                whole(2 * block, block),
                whole(block, 2 * block),
                column(1),
                column(block),
                column(taps),
                *[column(block) for _ in blocks],
                *[pl.BlockSpec(memory_space=pl.ANY) for _ in deps],
            ],
            out_specs=[pl.BlockSpec((chans, few, tile), lambda i, *_: (0, 0, i))] * 2,
        ),
        out_shape=[jax.ShapeDtypeStruct((chans, few, width), BF16)] * 2,
        cost_estimate=pl.CostEstimate(
            flops=2 * (3 * lags + 3) * 2 * block * block * width,
            bytes_accessed=2 * width * (taps + (len(blocks) + 2) * block),
            transcendentals=0,
        ),
        name="conv",
    )(
        core.reshape(1),
        jnp.asarray(forth, BF16),
        jnp.asarray(forth.T, BF16),
        skip.reshape(1, width),
        gates,
        filters,
        *blocks,
        *deps,
    )


def join_kernel(count, *refs):
    out_ref = refs[-1]
    start = 0
    for ref in refs[:count]:
        out_ref[start : start + ref.shape[0], :] = ref[...]
        start += ref.shape[0]


def join(parts, cols, deps=()):
    rows = sum(array.shape[0] for array, _ in parts)
    return pl.pallas_call(
        functools.partial(join_kernel, len(parts)),
        grid=(1,),
        in_specs=[
            *[
                pl.BlockSpec((array.shape[0], cols), lambda i, index=index: (0, index))
                for array, index in parts
            ],
            *[pl.BlockSpec(memory_space=pl.ANY) for _ in deps],
        ],
        out_specs=pl.BlockSpec((rows, cols), lambda i: (0, 0)),
        out_shape=jax.ShapeDtypeStruct((rows, cols), BF16),
        compiler_params=pltpu.CompilerParams(vmem_limit_bytes=12 * 2**20),
        name="join",
    )(*[array for array, _ in parts], *deps)


def part_kernel(many, slots, order_ref, from_ref, *refs):
    width = from_ref.shape[2] // slots
    for step, ref in enumerate(refs):
        here = order_ref[slots] ^ step
        if width % 128:
            ref[...] = from_ref[here]
            continue
        for slot in range(slots):
            start = pl.multiple_of(order_ref[slot] * width, width)
            ref[:, slot * width : (slot + 1) * width] = from_ref[here, :, pl.ds(start, width)]


def part(order, array):
    many, rows, depth = array.shape
    slots = order.shape[0] - 1
    width = depth // slots
    if width % 128:
        array = jnp.concatenate(
            [
                lax.dynamic_slice_in_dim(array, order[slot] * width, width, axis=2)
                for slot in range(slots)
            ],
            axis=2,
        )
    return list(
        pl.pallas_call(
            functools.partial(part_kernel, many, slots),
            grid_spec=pltpu.PrefetchScalarGridSpec(
                num_scalar_prefetch=1,
                grid=(1,),
                in_specs=[pl.BlockSpec(array.shape, lambda i, *_: (0, 0, 0))],
                out_specs=[pl.BlockSpec((rows, depth), lambda i, *_: (0, 0))] * many,
            ),
            out_shape=[jax.ShapeDtypeStruct((rows, depth), BF16)] * many,
            compiler_params=pltpu.CompilerParams(vmem_limit_bytes=12 * 2**20),
            name="part",
        )(order, array)
    )


def fence_kernel(*refs):
    del refs


def fence(arrays, deps):
    anywhere = pl.BlockSpec(memory_space=pl.ANY)
    return pl.pallas_call(
        fence_kernel,
        in_specs=[anywhere] * (len(arrays) + len(deps)),
        out_specs=[anywhere] * len(arrays),
        out_shape=[jax.ShapeDtypeStruct(array.shape, array.dtype) for array in arrays],
        input_output_aliases={index: index for index in range(len(arrays))},
        compiler_params=pltpu.CompilerParams(vmem_limit_bytes=2**20),
        name="fence",
    )(*arrays, *deps)


def project_kernel(count, firsts, tile, spots, width, *refs):
    act_refs, piece_refs = refs[:count], refs[count : count + len(firsts)]
    send_ref, keep_ref = refs[-2:]
    rows, cols = send_ref.shape
    acts = jnp.concatenate([act[...] for act in act_refs], axis=0)
    for start in range(0, cols, tile):
        weight = jnp.concatenate(
            [
                piece_refs[piece][
                    spot * width : (spot + 1) * width,
                    firsts[piece] * cols + start : firsts[piece] * cols + start + tile,
                ]
                for piece, spot in spots
            ],
            axis=0,
        )
        total = jnp.dot(acts, weight, preferred_element_type=F32)
        send_ref[:, start : start + tile] = total[:rows].astype(BF16)
        keep_ref[:, start : start + tile] = total[rows:]


def project(acts, pieces, spots, width, cols, deps):
    rows, depth = acts[0].shape
    count = rows * len(acts)
    tile = min(cols, 1024)
    firsts = [first for _, first in pieces]
    held = pl.BlockSpec(memory_space=pltpu.VMEM)
    return pl.pallas_call(
        functools.partial(project_kernel, len(acts), firsts, tile, spots, width),
        in_specs=[held] * (len(acts) + len(pieces))
        + [pl.BlockSpec(memory_space=pl.ANY)] * len(deps),
        out_specs=[held] * 2,
        out_shape=[
            jax.ShapeDtypeStruct((count // 2, cols), BF16),
            jax.ShapeDtypeStruct((count // 2, cols), F32),
        ],
        compiler_params=pltpu.CompilerParams(vmem_limit_bytes=16 * 2**20),
        cost_estimate=pl.CostEstimate(
            flops=2 * count * depth * cols,
            bytes_accessed=2 * depth * cols + 6 * count * cols,
            transcendentals=0,
        ),
        name="project",
    )(*acts, *[piece for piece, _ in pieces], *deps)


def body(values, gates, filters, skip, out_weight):
    pairs, chans = sizes()
    seq, chan = lax.axis_index("seq"), lax.axis_index("chan")
    pair, core = seq // 2, seq % 2
    block = values.shape[0]
    lags = filters.shape[0] // block
    own_rows, model = out_weight.shape
    half = model // 2
    rows = block // chans

    def swap(array):
        return permute(array, lambda p, k, c: (p, 1 - k, c))

    direct = [values]
    for _ in range(lags // 2):
        direct.append(permute(direct[-1], lambda p, k, c: (p + 1, k, c)))
    crossed = [
        permute(
            held,
            lambda p, k, c, first=index == 0, last=index == lags // 2: None
            if (first and k == 1) or (last and k == 0)
            else (p, 1 - k, c),
        )
        for index, held in enumerate(direct)
    ]

    bits = [1 << index for index in range(chans.bit_length() - 1)]
    parts, spots = [], []
    for which, order in enumerate((bits, bits[::-1])):
        held = join([(out_weight, which)], half)
        found = [0]
        for step, bit in enumerate(order):
            if step:
                held = join([(piece, 0) for piece in pieces], half)
            pieces = [held, permute(held, lambda p, k, c, bit=bit: (p, k, c ^ bit))]
            found = found + [mask ^ bit for mask in found]
        parts.append(pieces)
        each = len(found) // 2
        spots.append(
            [
                (2 * other + found.index(mask) // each, found.index(mask) % each)
                for other in range(2)
                for mask in range(chans)
            ]
        )

    gated = convolve(core, gates, filters, skip, direct, crossed, [])

    spreads = [lax.all_to_all(some, "chan", split_axis=0, concat_axis=0) for some in gated]

    flat = fence([piece for pieces in parts for piece in pieces], gated[:1])
    swaps = [swap(piece) for piece in flat]
    parts = [[*flat[at : at + 2], *swaps[at : at + 2]] for at in (0, 2)]
    spreads = [fence([some], swaps)[0] for some in spreads]
    order = [which * chans + (chan ^ mask) for which in (core, 1 - core) for mask in range(chans)]
    order = jnp.stack([*order, pair]).astype(jnp.int32)
    acts = []
    for spread in spreads:
        some = part(order, spread)
        for step in range(1, pairs):
            some[step] = permute(some[step], lambda p, k, c, step=step: (p ^ step, k, c))
        acts.append(some)

    count = pairs.bit_length() - 1
    steps = [1 << index for index in range(count)]
    ranks = sorted(range(pairs), key=lambda e: [not e & step for step in steps])
    acts = [[some[rank] for rank in ranks] for some in acts]

    outs = []
    passed = []
    for turn, some in enumerate(acts):
        row, sent = [], []
        for which in range(2):
            chunks = 2 if turn == 1 and which == 0 else 1
            for chunk in range(chunks):
                send, keep = project(
                    some,
                    [(piece, chunk) for piece in parts[which]],
                    spots[which],
                    own_rows,
                    half // chunks,
                    passed[:1] if which == 0 else [],
                )
                for index, step in enumerate(steps):
                    got = permute(send, lambda p, k, c, step=step: (p ^ step, k, c)).astype(F32)
                    many = got.shape[0] // 2
                    if index + 1 < count:
                        send = (keep[:many] + got[:many]).astype(BF16)
                        sent.append(send)
                        keep = keep[many:] + got[many:]
                    else:
                        keep = keep + got
                row.append(keep.astype(BF16))
        passed = sent
        outs.append(jnp.concatenate(row, axis=1))
    return jnp.concatenate(outs, axis=0)


def solution(mesh):
    in_specs = (
        P("seq", "chan"),
        P("seq", "chan"),
        P(None, "chan"),
        P("chan"),
        P(("seq", "chan"), None),
    )
    out_specs = P(("seq", "chan"), None)
    return jax.shard_map(body, mesh=mesh, in_specs=in_specs, out_specs=out_specs, check_vma=False)
```
